32 devices in a mesh: head: 4 (over x, core), blk: 8 (over z, y).
Axes of the slice: x: 2, y: 2, z: 4, core: 2. Of those that a mesh axis runs over, the one named last changes fastest.
Arguments:
- query: bfloat16 [4096, 8192], P(('blk', 'head'))
- key: bfloat16 [4096, 1024], P(('blk', 'head'))
- value: bfloat16 [4096, 1024], P(('blk', 'head')), may hold values from -6 to 6
- output_gradient: bfloat16 [4096, 8192], P(('blk', 'head')), may hold values from -6 to 6
- pair_codes: int32 [8, 8, 8], P('blk'), may hold values from 0 to 15
- pair_counts: int32 [8, 8], P('blk'), may hold values from 1 to 8
Outputs:
- attn_out: bfloat16 [4096, 8192], P(('blk', 'head'))
- grad_query: bfloat16 [4096, 8192], P(('blk', 'head'))
- key_gradient: bfloat16 [4096, 1024], P(('blk', 'head'))
- value_gradient: bfloat16 [4096, 1024], P(('blk', 'head'))
The draws below stay inside these ranges and needn't reach their ends.
All inputs are finite; a program needn't handle non-finite values.
Results may differ from the reference program's by a relative error of at most 0.015.
Values may be sent and summed in bfloat16 or wider, within the bound.
A program may use at most 128 MiB of HBM per device.

```python
import jax
import jax.numpy as jnp
import numpy as np
from jax import lax

QUERY_HEADS = 64
KEY_VALUE_HEADS = 8
HEAD_SIZE = 128
BLOCK = 128
NSTEP = 8
NB = 4
CAP = 8
SEQUENCE_TOKENS = 4096
N_BLK = 8


def drawn(key):
    base = jax.random.fold_in(key, 11)
    key_query, random_key_streams = jax.random.split(base, 2)
    queries = jnp.clip(jax.random.normal(key_query, (SEQUENCE_TOKENS, QUERY_HEADS * HEAD_SIZE), jnp.float32), -4.0, 4.0)
    key_tensor = jnp.clip(jax.random.normal(random_key_streams, (SEQUENCE_TOKENS, KEY_VALUE_HEADS * HEAD_SIZE), jnp.float32), -4.0, 4.0)
    return (queries, key_tensor)


def draw_query(key, part):
    return drawn(key)[0].astype(jnp.bfloat16)


def draw_key(key, part):
    return drawn(key)[1].astype(jnp.bfloat16)


def pattern(key):
    base = jax.random.fold_in(key, 29)
    key_level, key_extra, key_star, key_perm, key_lower = jax.random.split(base, 5)
    level = jax.random.randint(key_level, (N_BLK,), 1, 4)
    extra = jax.random.randint(key_extra, (N_BLK, NSTEP), 1, 5)
    steps_at = jnp.arange(NSTEP, dtype=jnp.int32)[None, :]
    groups_at = jnp.arange(N_BLK, dtype=jnp.int32)[:, None]
    counts = jnp.minimum(jnp.minimum(extra, 2 * level[:, None]), CAP)
    counts = jnp.where(steps_at == 0, NB + jnp.minimum(extra, level[:, None]), counts)
    star = jax.random.randint(key_star, (), 1, N_BLK)
    forced = jnp.logical_and(groups_at == star, steps_at == 1)
    counts = jnp.where(forced, CAP, counts)
    perm_keys = jax.random.split(key_perm, N_BLK * NSTEP)
    perms = jax.vmap(lambda single: jax.random.permutation(single, NB * NB))(perm_keys)
    codes = perms[:, :CAP].reshape(N_BLK, NSTEP, CAP).astype(jnp.int32)
    lower_table = np.array([row * NB + col for row in range(NB) for col in range(row)], dtype=np.int32)
    lower_keys = jax.random.split(key_lower, N_BLK)
    lower_perm = jax.vmap(lambda single: jax.random.permutation(single, lower_table.shape[0]))(lower_keys)
    lower_codes = jnp.asarray(lower_table)[lower_perm[:, :CAP - NB]]
    diagonal = jnp.broadcast_to(jnp.arange(NB, dtype=jnp.int32) * (NB + 1), (N_BLK, NB))
    first = jnp.concatenate([diagonal, lower_codes.astype(jnp.int32)], axis=1)
    codes = codes.at[:, 0, :].set(first)
    descending = (NB * NB - 1 - jnp.arange(CAP, dtype=jnp.int32))[None, None, :]
    codes = jnp.where(forced[:, :, None], descending, codes)
    return (codes.astype(jnp.int32), counts.astype(jnp.int32))


def draw_pair_codes(key, part):
    return pattern(key)[0]


def draw_pair_counts(key, part):
    return pattern(key)[1]


def steps_of(stream_key, extent, cuts, least, top_value):
    def one(axis_at, blocks):
        draws = jax.random.uniform(jax.random.fold_in(jax.random.fold_in(stream_key, 6), axis_at), (blocks,), jnp.float32, least / len(cuts), top_value / len(cuts))
        return jnp.repeat(jnp.exp(draws), extent[axis_at] // blocks).reshape((-1,) + (1,) * (len(extent) - axis_at - 1))

    loudness = one(*cuts[0])
    for cut in cuts[1:]:
        loudness = loudness * one(*cut)
    return loudness


def normal_values(key, shape, deviation, bound, cuts=(), held_as=jnp.bfloat16):
    loudness = steps_of(key, shape, cuts, -0.22, 0.18) if cuts else 1.0
    entries = jax.random.normal(key, shape, jnp.float32) * deviation * loudness
    return jnp.minimum(jnp.maximum(entries, -bound), bound).astype(held_as)


def setup_inputs(seed: int = 0) -> dict:
    splits = jax.random.split(jax.random.key(seed), 7)
    return {
        "query": draw_query(jax.random.fold_in(splits[6], 71), 0),
        "key": draw_key(jax.random.fold_in(splits[6], 71), 0),
        "value": normal_values(splits[2], (SEQUENCE_TOKENS, KEY_VALUE_HEADS * HEAD_SIZE), 1.0, 6.0, ((0, 32),)),
        "output_gradient": normal_values(splits[3], (SEQUENCE_TOKENS, QUERY_HEADS * HEAD_SIZE), 1.0, 6.0, ((0, 32),)),
        "pair_codes": draw_pair_codes(jax.random.fold_in(splits[6], 71), 0),
        "pair_counts": draw_pair_counts(jax.random.fold_in(splits[6], 71), 0),
    }


NEGATIVE_FILL = -1e30


def block_scores(q_blk, k_blk, query_block, key_block, first_step, score_scale):
    scores = jnp.einsum("qhgd,khd->hgqk", q_blk.astype(jnp.float32), k_blk.astype(jnp.float32)) * score_scale
    if first_step:
        rows_at = lax.broadcasted_iota(jnp.int32, scores.shape, 2)
        cols_at = lax.broadcasted_iota(jnp.int32, scores.shape, 3)
        allowed = jnp.logical_or(key_block != query_block, cols_at <= rows_at)
        scores = jnp.where(allowed, scores, NEGATIVE_FILL)
    return scores


def forward_pairs(loop_state, queries, key_tensor, values, codes, count, first_step, score_scale):
    def visit(index, carry):
        best, total, acc = carry
        code = codes[index]
        query_block = code // NB
        key_block = code % NB
        q_blk = lax.dynamic_slice_in_dim(queries, query_block * BLOCK, BLOCK, 0)
        k_blk = lax.dynamic_slice_in_dim(key_tensor, key_block * BLOCK, BLOCK, 0)
        v_blk = lax.dynamic_slice_in_dim(values, key_block * BLOCK, BLOCK, 0)
        scores = block_scores(q_blk, k_blk, query_block, key_block, first_step, score_scale)
        best_old = lax.dynamic_slice_in_dim(best, query_block * BLOCK, BLOCK, 2)
        total_old = lax.dynamic_slice_in_dim(total, query_block * BLOCK, BLOCK, 2)
        acc_old = lax.dynamic_slice_in_dim(acc, query_block * BLOCK, BLOCK, 0)
        best_new = jnp.maximum(best_old, jnp.max(scores, axis=-1))
        factor = jnp.exp(best_old - best_new)
        weights = jnp.exp(scores - best_new[..., None])
        total_new = factor * total_old + jnp.sum(weights, axis=-1)
        low = weights.astype(jnp.bfloat16).astype(jnp.float32)
        mixed = jnp.einsum("hgqk,khd->qhgd", low, v_blk.astype(jnp.float32))
        acc_new = jnp.transpose(factor, (2, 0, 1))[..., None] * acc_old + mixed
        best = lax.dynamic_update_slice_in_dim(best, best_new, query_block * BLOCK, 2)
        total = lax.dynamic_update_slice_in_dim(total, total_new, query_block * BLOCK, 2)
        acc = lax.dynamic_update_slice_in_dim(acc, acc_new, query_block * BLOCK, 0)
        return best, total, acc

    return lax.fori_loop(0, count, visit, loop_state)


def backward_pairs(loop_state, queries, grads, key_tensor, values, log_total, row_dot, codes, count, first_step, score_scale):
    def visit(index, carry):
        query_gradient, key_grad, value_grad = carry
        code = codes[index]
        query_block = code // NB
        key_block = code % NB
        q_blk = lax.dynamic_slice_in_dim(queries, query_block * BLOCK, BLOCK, 0)
        g_blk = lax.dynamic_slice_in_dim(grads, query_block * BLOCK, BLOCK, 0).astype(jnp.float32)
        k_blk = lax.dynamic_slice_in_dim(key_tensor, key_block * BLOCK, BLOCK, 0)
        v_blk = lax.dynamic_slice_in_dim(values, key_block * BLOCK, BLOCK, 0).astype(jnp.float32)
        scores = block_scores(q_blk, k_blk, query_block, key_block, first_step, score_scale)
        lse_blk = lax.dynamic_slice_in_dim(log_total, query_block * BLOCK, BLOCK, 2)
        row_blk = lax.dynamic_slice_in_dim(row_dot, query_block * BLOCK, BLOCK, 2)
        prob = jnp.exp(scores - lse_blk[..., None])
        low = prob.astype(jnp.bfloat16).astype(jnp.float32)
        value_part = jnp.einsum("hgqk,qhgd->khd", low, g_blk)
        dprob = jnp.einsum("qhgd,khd->hgqk", g_blk, v_blk)
        dscore = (prob * (dprob - row_blk[..., None])).astype(jnp.bfloat16).astype(jnp.float32)
        query_part = jnp.einsum("hgqk,khd->qhgd", dscore, k_blk.astype(jnp.float32))
        key_part = jnp.einsum("hgqk,qhgd->khd", dscore, q_blk.astype(jnp.float32))
        old_query = lax.dynamic_slice_in_dim(query_gradient, query_block * BLOCK, BLOCK, 0)
        query_gradient = lax.dynamic_update_slice_in_dim(query_gradient, old_query + query_part, query_block * BLOCK, 0)
        old_key = lax.dynamic_slice_in_dim(key_grad, key_block * BLOCK, BLOCK, 0)
        key_grad = lax.dynamic_update_slice_in_dim(key_grad, old_key + key_part, key_block * BLOCK, 0)
        old_value = lax.dynamic_slice_in_dim(value_grad, key_block * BLOCK, BLOCK, 0)
        value_grad = lax.dynamic_update_slice_in_dim(value_grad, old_value + value_part, key_block * BLOCK, 0)
        return query_gradient, key_grad, value_grad

    return lax.fori_loop(0, count, visit, loop_state)


def reference(query, key, value, output_gradient, pair_codes, pair_counts):
    device_sharding = QUERY_HEADS // KEY_VALUE_HEADS
    row_count_local = NB * BLOCK
    score_scale = HEAD_SIZE ** -0.5
    gathered_queries = query.reshape(N_BLK, row_count_local, KEY_VALUE_HEADS, device_sharding, HEAD_SIZE)
    gathered_gradients = output_gradient.reshape(N_BLK, row_count_local, KEY_VALUE_HEADS, device_sharding, HEAD_SIZE)
    gathered_keys = key.reshape(N_BLK, row_count_local, KEY_VALUE_HEADS, HEAD_SIZE)
    gathered_values = value.reshape(N_BLK, row_count_local, KEY_VALUE_HEADS, HEAD_SIZE)
    steps_range = jnp.arange(NSTEP, dtype=jnp.int32)

    def one_group(carry, inputs):
        key_gradient_sum, value_gradient_sum = carry
        queries, grads, codes, counts, group = inputs
        window = (group - steps_range) % N_BLK
        loop_state = (jnp.full((KEY_VALUE_HEADS, device_sharding, row_count_local), NEGATIVE_FILL, jnp.float32),
                 jnp.zeros((KEY_VALUE_HEADS, device_sharding, row_count_local), jnp.float32),
                 jnp.zeros((row_count_local, KEY_VALUE_HEADS, device_sharding, HEAD_SIZE), jnp.float32))
        for step in range(NSTEP):
            loop_state = forward_pairs(loop_state, queries, gathered_keys[window[step]], gathered_values[window[step]],
                                  codes[step], counts[step], step == 0, score_scale)
        best, total, acc = loop_state
        attn = (acc / jnp.transpose(total, (2, 0, 1))[..., None]).astype(jnp.bfloat16)
        log_total = best + jnp.log(total)
        row_dot = jnp.einsum("qhgd,qhgd->hgq", grads.astype(jnp.float32), attn.astype(jnp.float32))
        query_gradient = jnp.zeros((row_count_local, KEY_VALUE_HEADS, device_sharding, HEAD_SIZE), jnp.float32)
        for step in range(NSTEP):
            empty_key_value = jnp.zeros((row_count_local, KEY_VALUE_HEADS, HEAD_SIZE), jnp.float32)
            query_gradient, key_part, value_part = backward_pairs(
                (query_gradient, empty_key_value, empty_key_value), queries, grads, gathered_keys[window[step]],
                gathered_values[window[step]], log_total, row_dot, codes[step], counts[step], step == 0, score_scale)
            key_gradient_sum = key_gradient_sum.at[window[step]].add(key_part)
            value_gradient_sum = value_gradient_sum.at[window[step]].add(value_part)
        query_out = (query_gradient * score_scale).astype(jnp.bfloat16)
        return (key_gradient_sum, value_gradient_sum), (attn, query_out)

    start_offset = (jnp.zeros((N_BLK, row_count_local, KEY_VALUE_HEADS, HEAD_SIZE), jnp.float32), jnp.zeros((N_BLK, row_count_local, KEY_VALUE_HEADS, HEAD_SIZE), jnp.float32))
    groups = jnp.arange(N_BLK, dtype=jnp.int32)
    (key_gradient_sum, value_gradient_sum), (attn, query_out) = lax.scan(
        one_group, start_offset, (gathered_queries, gathered_gradients, pair_codes, pair_counts, groups))
    attn_out = attn.reshape(SEQUENCE_TOKENS, QUERY_HEADS * HEAD_SIZE)
    grad_query = query_out.reshape(SEQUENCE_TOKENS, QUERY_HEADS * HEAD_SIZE)
    key_gradient = (key_gradient_sum * score_scale).astype(jnp.bfloat16).reshape(SEQUENCE_TOKENS, KEY_VALUE_HEADS * HEAD_SIZE)
    value_gradient = value_gradient_sum.astype(jnp.bfloat16).reshape(SEQUENCE_TOKENS, KEY_VALUE_HEADS * HEAD_SIZE)
    return (attn_out, grad_query, key_gradient, value_gradient)
```

```python
import functools
import math

import jax
import jax.numpy as jnp
from jax import lax
from jax.experimental import pallas as pl
from jax.experimental.pallas import tpu as pltpu
from jax.sharding import PartitionSpec as P

KEY_VALUE_HEADS = 8
HEAD_SIZE = 128
BLOCK = 128
NEGATIVE_FILL = -1e30

NT = (((1,), (1,)), ((), ()))
NN = (((1,), (0,)), ((), ()))
TN = (((0,), (0,)), ((), ()))


def dot(a, b, dims):
    return lax.dot_general(a, b, dims, preferred_element_type=jnp.float32)


def attend(
    nstep, nblocks, heads, base_ref, codes_ref, counts_ref,
    q_ref, g_ref, kv_ref, out_ref, dkv_ref,
    lst, cnt, qs, gs, scores, out_t, dq_t, dk, dv,
):
    scale = HEAD_SIZE ** (-0.5)
    c2 = scale * math.log2(math.e)
    qb = pl.program_id(0)
    width = heads * BLOCK

    @pl.when(qb == 0)
    def _():
        dk[...] = jnp.zeros_like(dk)
        dv[...] = jnp.zeros_like(dv)
        base = base_ref[0]
        for b in range(nblocks):
            cnt[b] = 1
            lst[b * nstep * nblocks] = lax.rem(base, nstep) * nblocks + b

        def over_steps(s, _):
            place = lax.rem(base - s + nstep, nstep) * nblocks

            def over_codes(i, _):
                code = codes_ref[s, i]
                row = code // nblocks
                col = code - row * nblocks

                @pl.when(jnp.logical_or(s != 0, row != col))
                def _():
                    n = cnt[row]
                    lst[row * nstep * nblocks + n] = place + col
                    cnt[row] = n + 1

                return 0

            return lax.fori_loop(0, counts_ref[s], over_codes, 0)

        lax.fori_loop(0, nstep, over_steps, 0)

    n = cnt[qb]
    first = qb * nstep * nblocks

    def rows_of(i):
        return pl.ds(pl.multiple_of(lst[first + i] * BLOCK, BLOCK), BLOCK)

    for h in range(heads):
        cols = slice(h * BLOCK, (h + 1) * BLOCK)
        qs[cols, :] = q_ref[:, cols]
        gs[cols, :] = g_ref[:, cols]

    key_at = lax.broadcasted_iota(jnp.int32, (BLOCK, width), 0)
    query_at = lax.broadcasted_iota(jnp.int32, (BLOCK, width), 1) % BLOCK
    s0 = dot(kv_ref[rows_of(0), :HEAD_SIZE], qs[...], NT)
    s0 = jnp.where(key_at <= query_at, s0, NEGATIVE_FILL)
    scores[0] = s0
    top = jnp.max(s0, axis=0, keepdims=True)

    def score_pass(i, top):
        s = dot(kv_ref[rows_of(i), :HEAD_SIZE], qs[...], NT)
        scores[i] = s
        return jnp.maximum(top, jnp.max(s, axis=0, keepdims=True))

    top = lax.fori_loop(1, n, score_pass, top)
    out_t[...] = jnp.zeros_like(out_t)

    def weight_pass(i, total):
        w = jnp.exp2((scores[i] - top) * c2)
        scores[i] = w
        out_t[...] += dot(kv_ref[rows_of(i), HEAD_SIZE:], w.astype(jnp.bfloat16), TN)
        return total + jnp.sum(w, axis=0, keepdims=True)

    total = lax.fori_loop(0, n, weight_pass, jnp.zeros((1, width), jnp.float32))
    inv = 1.0 / total

    row_dots = []
    for h in range(heads):
        cols = slice(h * BLOCK, (h + 1) * BLOCK)
        attn = jnp.transpose(out_t[:, cols] * inv[:, cols]).astype(jnp.bfloat16)
        out_ref[:, cols] = attn
        prod = attn.astype(jnp.float32) * g_ref[:, cols].astype(jnp.float32)
        row_dots.append(jnp.sum(jnp.transpose(prod), axis=0, keepdims=True))
    row_dot = jnp.concatenate(row_dots, axis=1)
    dq_t[...] = jnp.zeros_like(dq_t)

    def grad_pass(i, _):
        rows = rows_of(i)
        p = scores[i] * inv
        dv[rows, :] += dot(p.astype(jnp.bfloat16), gs[...], NN)
        dp = dot(kv_ref[rows, HEAD_SIZE:], gs[...], NT)
        ds = (p * (dp - row_dot)).astype(jnp.bfloat16)
        dk[rows, :] += dot(ds, qs[...], NN)
        dq_t[...] += dot(kv_ref[rows, :HEAD_SIZE], ds, TN)
        return 0

    lax.fori_loop(0, n, grad_pass, 0)
    for h in range(heads):
        cols = slice(h * BLOCK, (h + 1) * BLOCK)
        out_ref[:, width + h * BLOCK : width + (h + 1) * BLOCK] = jnp.transpose(
            dq_t[:, cols] * scale
        ).astype(jnp.bfloat16)

    @pl.when(qb == nblocks - 1)
    def _():
        dkv_ref[:, :HEAD_SIZE] = (dk[...] * scale).astype(jnp.bfloat16)
        dkv_ref[:, HEAD_SIZE:] = dv[...].astype(jnp.bfloat16)


def attention(base, codes, counts, qg, kv):
    nstep = codes.shape[0]
    rows, both = qg.shape
    width = both // 2
    heads = width // HEAD_SIZE
    nblocks = rows // BLOCK
    keys = kv.shape[0]
    f32, bf16 = jnp.float32, jnp.bfloat16
    flops = 6 * 2 * 30 * width * BLOCK * HEAD_SIZE
    return pl.pallas_call(
        functools.partial(attend, nstep, nblocks, heads),
        out_shape=(
            jax.ShapeDtypeStruct((rows, 2 * width), bf16),
            jax.ShapeDtypeStruct((keys, 2 * HEAD_SIZE), bf16),
        ),
        grid_spec=pltpu.PrefetchScalarGridSpec(
            num_scalar_prefetch=3,
            grid=(nblocks,),
            in_specs=[
                pl.BlockSpec((BLOCK, width), lambda i, *_: (i, 0)),
                pl.BlockSpec((BLOCK, width), lambda i, *_: (i, 1)),
                pl.BlockSpec((keys, 2 * HEAD_SIZE), lambda i, *_: (0, 0)),
            ],
            out_specs=[
                pl.BlockSpec((BLOCK, 2 * width), lambda i, *_: (i, 0)),
                pl.BlockSpec((keys, 2 * HEAD_SIZE), lambda i, *_: (0, 0)),
            ],
            scratch_shapes=[
                pltpu.SMEM((nblocks * nstep * nblocks,), jnp.int32),
                pltpu.SMEM((nblocks,), jnp.int32),
                pltpu.VMEM((width, HEAD_SIZE), bf16),
                pltpu.VMEM((width, HEAD_SIZE), bf16),
                pltpu.VMEM((nstep * nblocks, BLOCK, width), f32),
                pltpu.VMEM((HEAD_SIZE, width), f32),
                pltpu.VMEM((HEAD_SIZE, width), f32),
                pltpu.VMEM((keys, HEAD_SIZE), f32),
                pltpu.VMEM((keys, HEAD_SIZE), f32),
            ],
        ),
        compiler_params=pltpu.CompilerParams(vmem_limit_bytes=44 * 2**20),
        cost_estimate=pl.CostEstimate(
            flops=4 * flops, bytes_accessed=2**23, transcendentals=30 * width * BLOCK
        ),
    )(base, codes, counts, qg, qg, kv)


def permuted(block, axis, distance):
    size = lax.axis_size(axis)
    return lax.ppermute(block, axis, [(i, (i + distance) % size) for i in range(size)])


def body(query, key, value, output_gradient, pair_codes, pair_counts):
    rows = query.shape[0]
    nh = lax.axis_size("head")
    nblk = lax.axis_size("blk")
    kv_local = KEY_VALUE_HEADS // nh
    codes, counts = pair_codes[0], pair_counts[0]
    nstep = codes.shape[0]
    whole = nblk == nstep

    def swap(x):
        return lax.all_to_all(x, "head", split_axis=0, concat_axis=0, tiled=True)

    def per_head(x):
        return jnp.transpose(x.reshape(rows, nh, kv_local, -1), (2, 1, 0, 3))

    k_parts, v_parts, q_parts, g_parts = map(per_head, (key, value, query, output_gradient))
    kv = jnp.concatenate([k_parts, v_parts], axis=-1)
    kv = swap(jnp.transpose(kv, (1, 0, 2, 3)))
    qg = [
        swap(jnp.concatenate([q_parts[j], g_parts[j]], axis=-1)).reshape(nh * rows, -1)
        for j in range(kv_local)
    ]

    def window(block):
        if whole:
            return lax.all_gather(block, "blk", axis=0, tiled=True)
        return jnp.concatenate(
            [block] + [permuted(block, "blk", nstep - i) for i in range(1, nstep)], axis=0
        )

    def returned(grads):
        if whole:
            return lax.psum_scatter(grads, "blk", scatter_dimension=0, tiled=True)
        parts = grads.reshape(nstep, nh * rows, -1)
        total = parts[0].astype(jnp.float32)
        for i in range(1, nstep):
            total += permuted(parts[i], "blk", i - nstep).astype(jnp.float32)
        return total.astype(jnp.bfloat16)

    base = lax.axis_index("blk") if whole else jnp.int32(0)
    base = jnp.reshape(base, (1,)).astype(jnp.int32)
    outs, kv_grads = [], []
    for j in range(kv_local):
        home = kv[:, j].reshape(nh * rows, 2 * HEAD_SIZE)
        out, grads = attention(base, codes, counts, qg[j], window(home))
        outs.append(swap(out.reshape(nh, rows, -1)))
        kv_grads.append(returned(grads).reshape(nh, rows, 2, HEAD_SIZE))
    kv_grads = swap(jnp.stack(kv_grads, axis=1))

    def whole_rows(parts, width):
        return jnp.transpose(parts, (2, 0, 1, 3)).reshape(rows, width)

    width = query.shape[1]
    half = width // KEY_VALUE_HEADS
    outs = jnp.stack(outs, axis=1)
    attn_out = whole_rows(outs[..., :half], width)
    grad_query = whole_rows(outs[..., half:], width)
    key_gradient = whole_rows(kv_grads[..., 0, :], key.shape[1])
    value_gradient = whole_rows(kv_grads[..., 1, :], key.shape[1])
    return (attn_out, grad_query, key_gradient, value_gradient)


def solution(mesh):
    tokens = P(("blk", "head"), None)
    return jax.shard_map(
        body,
        mesh=mesh,
        in_specs=(tokens,) * 4 + (P("blk", None, None), P("blk", None)),
        out_specs=(tokens,) * 4,
        check_vma=False,
    )
```

```python
import functools
import math

import jax
import jax.numpy as jnp
from jax import lax
from jax.experimental import pallas as pl
from jax.experimental.pallas import tpu as pltpu
from jax.sharding import PartitionSpec as P

KEY_VALUE_HEADS = 8
HEAD_SIZE = 128
BLOCK = 128
NEGATIVE_FILL = -1e30

NT = (((1,), (1,)), ((), ()))
NN = (((1,), (0,)), ((), ()))
TN = (((0,), (0,)), ((), ()))
MESH = pl.DeviceIdType.MESH
LINE = 2


def dot(a, b, dims):
    return lax.dot_general(a, b, dims, preferred_element_type=jnp.float32)


def attend(
    nstep, nblocks, heads, base_ref, codes_ref, counts_ref,
    q_ref, g_ref, k_ref, v_ref, out_ref, dkv_ref,
    lst, cnt, qs, gs, scores, out_t, dq_t, dk, dv,
):
    scale = HEAD_SIZE ** (-0.5)
    c2 = scale * math.log2(math.e)
    qb = pl.program_id(0)
    width = heads * BLOCK

    @pl.when(qb == 0)
    def _():
        dk[...] = jnp.zeros_like(dk)
        dv[...] = jnp.zeros_like(dv)
        base = base_ref[0]
        for b in range(nblocks):
            cnt[b] = 1
            lst[b * nstep * nblocks] = lax.rem(base, nstep) * nblocks + b

        def over_steps(s, _):
            place = lax.rem(base - s + nstep, nstep) * nblocks

            def over_codes(i, _):
                code = codes_ref[s, i]
                row = code // nblocks
                col = code - row * nblocks

                @pl.when(jnp.logical_or(s != 0, row != col))
                def _():
                    n = cnt[row]
                    lst[row * nstep * nblocks + n] = place + col
                    cnt[row] = n + 1

                return 0

            return lax.fori_loop(0, counts_ref[s], over_codes, 0)

        lax.fori_loop(0, nstep, over_steps, 0)

    n = cnt[qb]
    first = qb * nstep * nblocks

    def rows_of(i):
        return pl.ds(pl.multiple_of(lst[first + i] * BLOCK, BLOCK), BLOCK)

    for h in range(heads):
        cols = slice(h * BLOCK, (h + 1) * BLOCK)
        qs[cols, :] = q_ref[:, cols]
        gs[cols, :] = g_ref[:, cols]

    key_at = lax.broadcasted_iota(jnp.int32, (BLOCK, width), 0)
    query_at = lax.broadcasted_iota(jnp.int32, (BLOCK, width), 1) % BLOCK
    s0 = dot(k_ref[rows_of(0), :], qs[...], NT)
    s0 = jnp.where(key_at <= query_at, s0, NEGATIVE_FILL)
    scores[0] = s0
    top = jnp.max(s0, axis=0, keepdims=True)

    def score_pass(i, top):
        s = dot(k_ref[rows_of(i), :], qs[...], NT)
        scores[i] = s
        return jnp.maximum(top, jnp.max(s, axis=0, keepdims=True))

    top = lax.fori_loop(1, n, score_pass, top)
    out_t[...] = jnp.zeros_like(out_t)

    def weight_pass(i, total):
        w = jnp.exp2((scores[i] - top) * c2)
        scores[i] = w
        out_t[...] += dot(v_ref[rows_of(i), :], w.astype(jnp.bfloat16), TN)
        return total + jnp.sum(w, axis=0, keepdims=True)

    total = lax.fori_loop(0, n, weight_pass, jnp.zeros((1, width), jnp.float32))
    inv = 1.0 / total

    row_dots = []
    for h in range(heads):
        cols = slice(h * BLOCK, (h + 1) * BLOCK)
        attn = jnp.transpose(out_t[:, cols] * inv[:, cols]).astype(jnp.bfloat16)
        out_ref[:, cols] = attn
        prod = attn.astype(jnp.float32) * g_ref[:, cols].astype(jnp.float32)
        row_dots.append(jnp.sum(jnp.transpose(prod), axis=0, keepdims=True))
    row_dot = jnp.concatenate(row_dots, axis=1)
    dq_t[...] = jnp.zeros_like(dq_t)

    def grad_pass(i, _):
        rows = rows_of(i)
        p = scores[i] * inv
        dv[rows, :] += dot(p.astype(jnp.bfloat16), gs[...], NN)
        dp = dot(v_ref[rows, :], gs[...], NT)
        ds = (p * (dp - row_dot)).astype(jnp.bfloat16)
        dk[rows, :] += dot(ds, qs[...], NN)
        dq_t[...] += dot(k_ref[rows, :], ds, TN)
        return 0

    lax.fori_loop(0, n, grad_pass, 0)
    for h in range(heads):
        cols = slice(h * BLOCK, (h + 1) * BLOCK)
        out_ref[:, width + h * BLOCK : width + (h + 1) * BLOCK] = jnp.transpose(
            dq_t[:, cols] * scale
        ).astype(jnp.bfloat16)

    @pl.when(qb == nblocks - 1)
    def _():
        dkv_ref[:, :HEAD_SIZE] = (dk[...] * scale).astype(jnp.bfloat16)
        dkv_ref[:, HEAD_SIZE:] = dv[...].astype(jnp.bfloat16)


def attention(j, kv_local, base, codes, counts, q, g, kv):
    nstep = codes.shape[0]
    rows = q.shape[0]
    width = q.shape[1] // kv_local
    heads = width // HEAD_SIZE
    nblocks = rows // BLOCK
    keys = kv.shape[0]
    f32, bf16 = jnp.float32, jnp.bfloat16
    flops = 6 * 2 * 30 * width * BLOCK * HEAD_SIZE
    return pl.pallas_call(
        functools.partial(attend, nstep, nblocks, heads),
        out_shape=(
            jax.ShapeDtypeStruct((rows, 2 * width), bf16),
            jax.ShapeDtypeStruct((keys, 2 * HEAD_SIZE), bf16),
        ),
        grid_spec=pltpu.PrefetchScalarGridSpec(
            num_scalar_prefetch=3,
            grid=(nblocks,),
            in_specs=[
                pl.BlockSpec((BLOCK, width), lambda i, *_: (i, j)),
                pl.BlockSpec((BLOCK, width), lambda i, *_: (i, j)),
                pl.BlockSpec((keys, HEAD_SIZE), lambda i, *_: (0, j)),
                pl.BlockSpec((keys, HEAD_SIZE), lambda i, *_: (0, kv_local + j)),
            ],
            out_specs=[
                pl.BlockSpec((BLOCK, 2 * width), lambda i, *_: (i, 0)),
                pl.BlockSpec((keys, 2 * HEAD_SIZE), lambda i, *_: (0, 0)),
            ],
            scratch_shapes=[
                pltpu.SMEM((nblocks * nstep * nblocks,), jnp.int32),
                pltpu.SMEM((nblocks,), jnp.int32),
                pltpu.VMEM((width, HEAD_SIZE), bf16),
                pltpu.VMEM((width, HEAD_SIZE), bf16),
                pltpu.VMEM((nstep * nblocks, BLOCK, width), f32),
                pltpu.VMEM((HEAD_SIZE, width), f32),
                pltpu.VMEM((HEAD_SIZE, width), f32),
                pltpu.VMEM((keys, HEAD_SIZE), f32),
                pltpu.VMEM((keys, HEAD_SIZE), f32),
            ],
        ),
        compiler_params=pltpu.CompilerParams(vmem_limit_bytes=44 * 2**20),
        cost_estimate=pl.CostEstimate(
            flops=4 * flops, bytes_accessed=2**23, transcendentals=30 * width * BLOCK
        ),
    )(base, codes, counts, q, g, kv, kv)


def greet(nh, nblk, whole, me, blk):
    barrier = pltpu.get_barrier_semaphore()
    for m in range(1, nh):
        pl.semaphore_signal(
            barrier, inc=1, device_id=(lax.rem(me + m, nh), blk), device_id_type=MESH
        )
    others = nblk if whole else 1
    for m in range(1, others):
        pl.semaphore_signal(
            barrier, inc=1, device_id=(me, lax.rem(blk + m, nblk)), device_id_type=MESH
        )
    pl.semaphore_wait(barrier, nh - 1 + others - 1)


def aligned(index, size):
    return pl.ds(pl.multiple_of(index * size, size), size)


def remote(src, dst, sems, device):
    return pltpu.make_async_remote_copy(
        src_ref=src, dst_ref=dst, send_sem=sems[0], recv_sem=sems[1],
        device_id=device, device_id_type=MESH,
    )


def enter(
    nh, nblk, whole, q, k, v, g, qo, go, kvo,
    send, recv, local, up_s, up_r, down_s, down_r, y_s, y_r,
):
    me, blk = lax.axis_index("head"), lax.axis_index("blk")
    greet(nh, nblk, whole, me, blk)
    rows = q.shape[0]
    qc, kc = q.shape[1] // nh, k.shape[1] // nh
    group = nh * rows
    home = blk * nh if whole else 0

    def parts(n):
        at = aligned(home + me, rows)
        mine = aligned(me, rows)
        return (
            (k, kc, kvo.at[at, pl.ds(0, kc)]),
            (v, kc, kvo.at[at, pl.ds(kc, kc)]),
            (q, qc, qo.at[mine, :]),
            (g, qc, go.at[mine, :]),
        )[n]

    def to_peer(n, m):
        src, cols, dst = parts(n)
        peer = lax.rem(me + m, nh)
        return remote(
            src.at[:, aligned(peer, cols)], dst,
            (send.at[n, m - 1], recv.at[n, m - 1]), (peer, blk),
        )

    def own(n):
        src, cols, dst = parts(n)
        return pltpu.make_async_copy(src.at[:, aligned(me, cols)], dst, local.at[n])

    order = (2, 3, 1) if nh == 4 else tuple(range(1, nh))
    for n in (0, 1):
        for m in order:
            to_peer(n, m).start()
        own(n).start()
    for n in (0, 1):
        for m in order:
            to_peer(n, m).wait_recv()
        own(n).wait()

    nz = nblk // LINE
    hi, lo = blk // LINE, lax.rem(blk, LINE)

    def block(z):
        return kvo.at[aligned(z * LINE + lo, group), :]

    def up(d):
        return remote(
            block(hi - d), block(hi - d), (up_s.at[d], up_r.at[d]), (me, blk + LINE)
        )

    def down(d):
        return remote(
            block(hi + d), block(hi + d), (down_s.at[d], down_r.at[d]), (me, blk - LINE)
        )

    def across(z, slot):
        return remote(
            block(z), block(z), (y_s.at[slot], y_r.at[slot]), (me, blk + 1 - 2 * lo)
        )

    def start_q():
        for n in (2, 3):
            for m in order:
                to_peer(n, m).start()
            own(n).start()

    if whole:
        for d in range(nz):
            if d > 0:
                pl.when(hi - d >= 0)(lambda d=d: block_wait(up, d - 1))
            if d < nz - 1:
                pl.when(jnp.logical_and(hi - d >= 0, hi < nz - 1))(lambda d=d: up(d).start())
            if d > 0:
                pl.when(hi + d < nz)(lambda d=d: block_wait(down, d - 1))
            if d < nz - 1:
                pl.when(jnp.logical_and(hi + d < nz, hi > 0))(lambda d=d: down(d).start())
            if d == 0:
                across(hi, 0).start()
                start_q()
            else:
                pl.when(hi - d >= 0)(lambda d=d: across(hi - d, d).start())
                pl.when(hi + d < nz)(lambda d=d: across(hi + d, nz - 1 + d).start())
        across(hi, 0).wait()
        for d in range(1, nz):
            pl.when(hi - d >= 0)(lambda d=d: across(hi - d, d).wait())
            pl.when(hi + d < nz)(lambda d=d: across(hi + d, nz - 1 + d).wait())
        for d in range(nz - 1):
            pl.when(jnp.logical_and(hi - d >= 0, hi < nz - 1))(lambda d=d: up(d).wait_send())
            pl.when(jnp.logical_and(hi + d < nz, hi > 0))(lambda d=d: down(d).wait_send())
    else:
        start_q()
    for n in (2, 3):
        for m in order:
            to_peer(n, m).wait_recv()
        own(n).wait()
    for n in range(4):
        for m in order:
            to_peer(n, m).wait_send()


def block_wait(copy, d):
    copy(d).wait_recv()


def leave(
    nh, nblk, whole, o0, o1, d0, d1, attn, dq, dk, dv,
    y_in, up_in, down_in, sums, home, send, recv, local,
    up_s, up_r, down_s, down_r, y_s, y_r,
):
    me, blk = lax.axis_index("head"), lax.axis_index("blk")
    greet(nh, nblk, whole, me, blk)
    outs, grads = (o0, o1), (d0, d1)
    rows = attn.shape[0]
    group = nh * rows
    half = o0.shape[1] // 2
    kw = d0.shape[1]
    kv_local = len(outs)
    f32, bf16 = jnp.float32, jnp.bfloat16
    nz = nblk // LINE
    hi, lo = blk // LINE, lax.rem(blk, LINE)

    def part(n, row):
        if n < 2 * kv_local:
            j, which = n // 2, n % 2
            return (
                outs[j].at[aligned(row, rows), pl.ds(which * half, half)],
                (attn, dq)[which].at[:, aligned(me * kv_local + j, half)],
            )
        which = n - 2 * kv_local
        return (
            home.at[aligned(row, rows), pl.ds(which * kw, kw)],
            (dk, dv)[which].at[:, aligned(me, kw)],
        )

    def to_peer(n, m):
        peer = lax.rem(me + m, nh)
        src, dst = part(n, peer)
        return remote(src, dst, (send.at[n, m - 1], recv.at[n, m - 1]), (peer, blk))

    def own(n):
        src, dst = part(n, me)
        return pltpu.make_async_copy(src, dst, local.at[n])

    order = (2, 3, 1) if nh == 4 else tuple(range(1, nh))
    count = 2 * kv_local

    def across(z, j):
        other = aligned(z * LINE + 1 - lo, group)
        return remote(
            grads[j].at[other, :], y_in.at[z, j], (y_s.at[z, j], y_r.at[z, j]),
            (me, blk + 1 - 2 * lo),
        )

    def start_outs():
        for n in range(count):
            for m in order:
                to_peer(n, m).start()
            own(n).start()

    def up(z):
        return remote(sums.at[z], up_in.at[z], (up_s.at[z], up_r.at[z]), (me, blk + LINE))

    def down(z):
        return remote(
            sums.at[z], down_in.at[z], (down_s.at[z], down_r.at[z]), (me, blk - LINE)
        )

    def keep(z, value):
        for j in range(kv_local):
            sums[z, j] = value[j].astype(bf16)

    def mine(z):
        at = aligned(z * LINE + lo, group)
        return [
            grads[j][at, :].astype(f32) + y_in[z, j].astype(f32) for j in range(kv_local)
        ]

    def with_in(value, arrived, z):
        return [value[j] + arrived[z, j].astype(f32) for j in range(kv_local)]

    def finish(value):
        for j in range(kv_local):
            for which in range(2):
                at = which * kv_local + j
                home[:, at * HEAD_SIZE : (at + 1) * HEAD_SIZE] = value[j][
                    :, which * HEAD_SIZE : (which + 1) * HEAD_SIZE
                ].astype(bf16)

    if whole:
        far_first = sorted(range(nz), key=lambda z: -abs(2 * z - nz + 1))
        for z in far_first:
            for j in range(kv_local):
                across(z, j).start()
        start_outs()
        for z in far_first:
            for j in range(kv_local):
                across(z, j).wait_recv()

            @pl.when(hi < z)
            def _(z=z):
                @pl.when(hi == 0)
                def _():
                    keep(z, mine(z))

                @pl.when(hi > 0)
                def _():
                    up(z).wait_recv()
                    keep(z, with_in(mine(z), up_in, z))

                up(z).start()

            @pl.when(hi > z)
            def _(z=z):
                @pl.when(hi == nz - 1)
                def _():
                    keep(z, mine(z))

                @pl.when(hi < nz - 1)
                def _():
                    down(z).wait_recv()
                    keep(z, with_in(mine(z), down_in, z))

                down(z).start()

        for z in range(nz):
            @pl.when(hi == z)
            def _(z=z):
                value = mine(z)
                if z > 0:
                    up(z).wait_recv()
                    value = with_in(value, up_in, z)
                if z < nz - 1:
                    down(z).wait_recv()
                    value = with_in(value, down_in, z)
                finish(value)

    else:
        start_outs()
        finish([grads[j][...].astype(f32) for j in range(kv_local)])
    for n in (count, count + 1):
        for m in order:
            to_peer(n, m).start()
        own(n).start()
    if whole:
        for z in range(nz):
            for j in range(kv_local):
                across(z, j).wait_send()
            pl.when(hi < z)(lambda z=z: up(z).wait_send())
            pl.when(hi > z)(lambda z=z: down(z).wait_send())
    for n in range(count + 2):
        for m in order:
            to_peer(n, m).wait()
        own(n).wait()


def permuted(block, axis, distance):
    size = lax.axis_size(axis)
    return lax.ppermute(block, axis, [(i, (i + distance) % size) for i in range(size)])


def body(query, key, value, output_gradient, pair_codes, pair_counts):
    rows = query.shape[0]
    nh = lax.axis_size("head")
    nblk = lax.axis_size("blk")
    kv_local = KEY_VALUE_HEADS // nh
    codes, counts = pair_codes[0], pair_counts[0]
    nstep = codes.shape[0]
    whole = nblk == nstep
    nz = nblk // LINE
    group = nh * rows
    bf16 = jnp.bfloat16
    dma = pltpu.SemaphoreType.DMA
    anywhere = pl.BlockSpec(memory_space=pl.ANY)
    in_vmem = pl.BlockSpec(memory_space=pltpu.VMEM)
    qw, kw = query.shape[1] // nh, key.shape[1] // nh
    keys = group * (nblk if whole else 1)
    q, g, kv = pl.pallas_call(
        functools.partial(enter, nh, nblk, whole),
        out_shape=(
            jax.ShapeDtypeStruct((group, qw), bf16),
            jax.ShapeDtypeStruct((group, qw), bf16),
            jax.ShapeDtypeStruct((keys, 2 * kw), bf16),
        ),
        in_specs=[anywhere] * 4,
        out_specs=[anywhere] * 3,
        scratch_shapes=[
            dma((4, nh - 1)), dma((4, nh - 1)), dma((4,)),
            dma((nz,)), dma((nz,)), dma((nz,)), dma((nz,)),
            dma((2 * nz,)), dma((2 * nz,)),
        ],
        compiler_params=pltpu.CompilerParams(collective_id=0, has_side_effects=True),
    )(query, key, value, output_gradient)
    if not whole:
        kv = jnp.concatenate(
            [kv] + [permuted(kv, "blk", nstep - i) for i in range(1, nstep)], axis=0
        )
    base = lax.axis_index("blk") if whole else jnp.int32(0)
    base = jnp.reshape(base, (1,)).astype(jnp.int32)
    outs, grads = [], []
    for j in range(kv_local):
        out, grad = attention(j, kv_local, base, codes, counts, q, g, kv)
        if not whole:
            parts = grad.reshape(nstep, group, -1)
            total = parts[0].astype(jnp.float32)
            for i in range(1, nstep):
                total += permuted(parts[i], "blk", i - nstep).astype(jnp.float32)
            grad = total.astype(bf16)
        outs.append(out)
        grads.append(grad)
    slots = (nz if whole else 1, kv_local, group, 2 * HEAD_SIZE)
    like = jax.ShapeDtypeStruct
    return pl.pallas_call(
        functools.partial(leave, nh, nblk, whole),
        out_shape=(
            like(query.shape, bf16), like(query.shape, bf16),
            like(key.shape, bf16), like(value.shape, bf16),
        ),
        in_specs=[anywhere] * 2 + [in_vmem] * 2,
        out_specs=[anywhere] * 4,
        scratch_shapes=[
            pltpu.VMEM(slots, bf16), pltpu.VMEM(slots, bf16), pltpu.VMEM(slots, bf16),
            pltpu.VMEM(slots, bf16), pltpu.VMEM((group, 2 * kw), bf16),
            dma((2 * kv_local + 2, nh - 1)), dma((2 * kv_local + 2, nh - 1)),
            dma((2 * kv_local + 2,)),
            dma((nz,)), dma((nz,)), dma((nz,)), dma((nz,)),
            dma((nz, kv_local)), dma((nz, kv_local)),
        ],
        compiler_params=pltpu.CompilerParams(
            collective_id=1, has_side_effects=True, vmem_limit_bytes=40 * 2**20
        ),
    )(*outs, *grads)


def solution(mesh):
    tokens = P(("blk", "head"), None)
    return jax.shard_map(
        body,
        mesh=mesh,
        in_specs=(tokens,) * 4 + (P("blk", None, None), P("blk", None)),
        out_specs=(tokens,) * 4,
        check_vma=False,
    )
```

```python
import functools
import math

import jax
import jax.numpy as jnp
from jax import lax
from jax.experimental import pallas as pl
from jax.experimental.pallas import tpu as pltpu
from jax.sharding import PartitionSpec as P

QUERY_HEADS = 64
KEY_VALUE_HEADS = 8
HEAD_SIZE = 128
BLOCK = 128
NEGATIVE_FILL = -1e30

NT = (((1,), (1,)), ((), ()))
NN = (((1,), (0,)), ((), ()))
TN = (((0,), (0,)), ((), ()))
MESH = pl.DeviceIdType.MESH
LINE = 2


def dot(a, b, dims):
    return lax.dot_general(a, b, dims, preferred_element_type=jnp.float32)


def query_block(nblocks, base_ref, turn):
    return lax.rem(base_ref[1] + base_ref[2] * turn, nblocks)


def attend(
    nstep, nblocks, heads, split, base_ref, codes_ref, counts_ref,
    q_ref, g_ref, k_ref, v_ref, out_ref, dkv_ref,
    lst, cnt, qs, gs, scores, out_t, dq_t, dk, dv,
):
    def place_of(base, s):
        at = lax.rem(base - s + nstep, nstep)
        if not split:
            return at
        far = lax.rem(at + base, LINE)
        return at // LINE + far * (nstep // LINE)

    scale = HEAD_SIZE ** (-0.5)
    c2 = scale * math.log2(math.e)
    turn = pl.program_id(0)
    qb = query_block(nblocks, base_ref, turn)
    width = heads * BLOCK

    @pl.when(turn == 0)
    def _():
        dk[...] = jnp.zeros_like(dk)
        dv[...] = jnp.zeros_like(dv)
        base = base_ref[0]
        for b in range(nblocks):
            cnt[b] = 1
            lst[b * nstep * nblocks] = place_of(base, 0) * nblocks + b

        def over_steps(s, _):
            place = place_of(base, s) * nblocks

            def over_codes(i, _):
                code = codes_ref[s, i]
                row = code // nblocks
                col = code - row * nblocks

                @pl.when(jnp.logical_or(s != 0, row != col))
                def _():
                    n = cnt[row]
                    lst[row * nstep * nblocks + n] = place + col
                    cnt[row] = n + 1

                return 0

            return lax.fori_loop(0, counts_ref[s], over_codes, 0)

        lax.fori_loop(0, nstep, over_steps, 0)

    n = cnt[qb]
    first = qb * nstep * nblocks

    def rows_of(i):
        return pl.ds(pl.multiple_of(lst[first + i] * BLOCK, BLOCK), BLOCK)

    for h in range(heads):
        cols = slice(h * BLOCK, (h + 1) * BLOCK)
        qs[cols, :] = q_ref[:, cols]
        gs[cols, :] = g_ref[:, cols]

    key_at = lax.broadcasted_iota(jnp.int32, (BLOCK, width), 0)
    query_at = lax.broadcasted_iota(jnp.int32, (BLOCK, width), 1) % BLOCK
    s0 = dot(k_ref[rows_of(0), :], qs[...], NT)
    s0 = jnp.where(key_at <= query_at, s0, NEGATIVE_FILL)
    scores[0] = s0
    top = jnp.max(s0, axis=0, keepdims=True)

    def score_pass(i, top):
        s = dot(k_ref[rows_of(i), :], qs[...], NT)
        scores[i] = s
        return jnp.maximum(top, jnp.max(s, axis=0, keepdims=True))

    top = lax.fori_loop(1, n, score_pass, top)
    out_t[...] = jnp.zeros_like(out_t)

    def weight_pass(i, total):
        w = jnp.exp2((scores[i] - top) * c2)
        scores[i] = w
        out_t[...] += dot(v_ref[rows_of(i), :], w.astype(jnp.bfloat16), TN)
        return total + jnp.sum(w, axis=0, keepdims=True)

    total = lax.fori_loop(0, n, weight_pass, jnp.zeros((1, width), jnp.float32))
    inv = 1.0 / total

    row_dots = []
    for h in range(heads):
        cols = slice(h * BLOCK, (h + 1) * BLOCK)
        attn = jnp.transpose(out_t[:, cols] * inv[:, cols]).astype(jnp.bfloat16)
        out_ref[:, cols] = attn
        prod = attn.astype(jnp.float32) * g_ref[:, cols].astype(jnp.float32)
        row_dots.append(jnp.sum(jnp.transpose(prod), axis=0, keepdims=True))
    row_dot = jnp.concatenate(row_dots, axis=1)
    dq_t[...] = jnp.zeros_like(dq_t)

    def grad_pass(i, _):
        rows = rows_of(i)
        p = scores[i] * inv
        dv[rows, :] += dot(p.astype(jnp.bfloat16), gs[...], NN)
        dp = dot(v_ref[rows, :], gs[...], NT)
        ds = (p * (dp - row_dot)).astype(jnp.bfloat16)
        dk[rows, :] += dot(ds, qs[...], NN)
        dq_t[...] += dot(k_ref[rows, :], ds, TN)
        return 0

    lax.fori_loop(0, n, grad_pass, 0)
    for h in range(heads):
        cols = slice(h * BLOCK, (h + 1) * BLOCK)
        out_ref[:, width + h * BLOCK : width + (h + 1) * BLOCK] = jnp.transpose(
            dq_t[:, cols] * scale
        ).astype(jnp.bfloat16)

    @pl.when(turn == nblocks - 1)
    def _():
        dkv_ref[:, :HEAD_SIZE] = (dk[...] * scale).astype(jnp.bfloat16)
        dkv_ref[:, HEAD_SIZE:] = dv[...].astype(jnp.bfloat16)


def attention(split, base, codes, counts, q, g, kv):
    nstep = codes.shape[0]
    rows = q.shape[0]
    width = HEAD_SIZE * (QUERY_HEADS // KEY_VALUE_HEADS)
    gcol = g.shape[1] // width - 1
    heads = width // HEAD_SIZE
    nblocks = rows // BLOCK
    keys = kv.shape[0]
    f32, bf16 = jnp.float32, jnp.bfloat16
    flops = 6 * 2 * 30 * width * BLOCK * HEAD_SIZE
    return pl.pallas_call(
        functools.partial(attend, nstep, nblocks, heads, split),
        out_shape=(
            jax.ShapeDtypeStruct((rows, 2 * width), bf16),
            jax.ShapeDtypeStruct((keys, 2 * HEAD_SIZE), bf16),
        ),
        grid_spec=pltpu.PrefetchScalarGridSpec(
            num_scalar_prefetch=3,
            grid=(nblocks,),
            in_specs=[
                pl.BlockSpec((BLOCK, width), lambda i, *_: (i, 0)),
                pl.BlockSpec((BLOCK, width), lambda i, *_: (i, gcol)),
                pl.BlockSpec((keys, HEAD_SIZE), lambda i, *_: (0, 0)),
                pl.BlockSpec((keys, HEAD_SIZE), lambda i, *_: (0, 1)),
            ],
            out_specs=[
                pl.BlockSpec(
                    (BLOCK, 2 * width),
                    lambda i, base, *_: (query_block(nblocks, base, i), 0),
                ),
                pl.BlockSpec((keys, 2 * HEAD_SIZE), lambda i, *_: (0, 0)),
            ],
            scratch_shapes=[
                pltpu.SMEM((nblocks * nstep * nblocks,), jnp.int32),
                pltpu.SMEM((nblocks,), jnp.int32),
                pltpu.VMEM((width, HEAD_SIZE), bf16),
                pltpu.VMEM((width, HEAD_SIZE), bf16),
                pltpu.VMEM((nstep * nblocks, BLOCK, width), f32),
                pltpu.VMEM((HEAD_SIZE, width), f32),
                pltpu.VMEM((HEAD_SIZE, width), f32),
                pltpu.VMEM((keys, HEAD_SIZE), f32),
                pltpu.VMEM((keys, HEAD_SIZE), f32),
            ],
        ),
        compiler_params=pltpu.CompilerParams(vmem_limit_bytes=44 * 2**20),
        cost_estimate=pl.CostEstimate(
            flops=16 * flops, bytes_accessed=2**23, transcendentals=30 * width * BLOCK
        ),
    )(base, codes, counts, q, g, kv, kv)


def greet(nh, nblk, whole, me, blk):
    barrier = pltpu.get_barrier_semaphore()
    for m in range(1, nh):
        pl.semaphore_signal(
            barrier, inc=1, device_id=(lax.rem(me + m, nh), blk), device_id_type=MESH
        )
    others = nblk if whole else 1
    for m in range(1, others):
        pl.semaphore_signal(
            barrier, inc=1, device_id=(me, lax.rem(blk + m, nblk)), device_id_type=MESH
        )
    pl.semaphore_wait(barrier, nh - 1 + others - 1)


def aligned(index, size):
    return pl.ds(pl.multiple_of(index * size, size), size)


def remote(src, dst, sems, device):
    return pltpu.make_async_remote_copy(
        src_ref=src, dst_ref=dst, send_sem=sems[0], recv_sem=sems[1],
        device_id=device, device_id_type=MESH,
    )


def enter(
    nh, nblk, whole, q, k, v, g, q0, g0, kv0, kv1,
    send, recv, local, up_s, up_r, down_s, down_r, y_s, y_r,
):
    me, blk = lax.axis_index("head"), lax.axis_index("blk")
    greet(nh, nblk, whole, me, blk)
    rows = q.shape[0]
    qc = q0.shape[1]
    group = nh * rows
    nz = nblk // LINE
    hi, lo = blk // LINE, lax.rem(blk, LINE)
    keys = (kv0, kv1)

    def parts(n):
        if n < 4:
            j, which = n // 2, n % 2
            at = aligned((hi * nh if whole else 0) + me, rows)
            dst = keys[j].at[at, pl.ds(which * HEAD_SIZE, HEAD_SIZE)]
            return (k, v)[which], HEAD_SIZE, j, dst
        return (q, g)[n - 4], qc, 0, (q0, g0)[n - 4].at[aligned(me, rows), :]

    def to_peer(n, m):
        src, cols, j, dst = parts(n)
        peer = lax.rem(me + m, nh)
        return remote(
            src.at[:, aligned(peer * 2 + j, cols)], dst,
            (send.at[n, m - 1], recv.at[n, m - 1]), (peer, blk),
        )

    def own(n):
        src, cols, j, dst = parts(n)
        return pltpu.make_async_copy(src.at[:, aligned(me * 2 + j, cols)], dst, local.at[n])

    order = (2, 3, 1) if nh == 4 else tuple(range(1, nh))

    def start(n):
        for m in order:
            to_peer(n, m).start()
        own(n).start()

    def arrived(n):
        for m in order:
            to_peer(n, m).wait_recv()
        own(n).wait()

    def block(j, z):
        return keys[j].at[aligned(z, group), :]

    def up(j, d):
        return remote(
            block(j, hi - d), block(j, hi - d), (up_s.at[j, d], up_r.at[j, d]),
            (me, blk + LINE),
        )

    def down(j, d):
        return remote(
            block(j, hi + d), block(j, hi + d), (down_s.at[j, d], down_r.at[j, d]),
            (me, blk - LINE),
        )

    def across(z, slot):
        return remote(
            block(0, z), block(0, nz + z), (y_s.at[slot], y_r.at[slot]),
            (me, blk + 1 - 2 * lo),
        )

    def pass_on(j, d):
        if d > 0:
            pl.when(hi - d >= 0)(lambda: up(j, d - 1).wait_recv())
        if d < nz - 1:
            pl.when(jnp.logical_and(hi - d >= 0, hi < nz - 1))(lambda: up(j, d).start())
        if d > 0:
            pl.when(hi + d < nz)(lambda: down(j, d - 1).wait_recv())
        if d < nz - 1:
            pl.when(jnp.logical_and(hi + d < nz, hi > 0))(lambda: down(j, d).start())
        if j > 0:
            return
        if d == 0:
            across(hi, 0).start()
        else:
            pl.when(hi - d >= 0)(lambda: across(hi - d, d).start())
            pl.when(hi + d < nz)(lambda: across(hi + d, nz - 1 + d).start())

    for n in range(4):
        start(n)
    for j in range(2):
        arrived(2 * j)
        arrived(2 * j + 1)
        if whole:
            pass_on(j, 0)
    start(4)
    start(5)
    if whole:
        for d in range(1, nz):
            pass_on(0, d)
            pass_on(1, d)
        across(hi, 0).wait()
        for d in range(1, nz):
            pl.when(hi - d >= 0)(lambda d=d: across(hi - d, d).wait())
            pl.when(hi + d < nz)(lambda d=d: across(hi + d, nz - 1 + d).wait())
        for j in range(2):
            for d in range(nz - 1):
                pl.when(jnp.logical_and(hi - d >= 0, hi < nz - 1))(
                    lambda j=j, d=d: up(j, d).wait_send()
                )
                pl.when(jnp.logical_and(hi + d < nz, hi > 0))(
                    lambda j=j, d=d: down(j, d).wait_send()
                )
    arrived(4)
    arrived(5)
    for n in range(6):
        for m in order:
            to_peer(n, m).wait_send()


def leave(
    nh, nblk, whole, o0, r1, r2, r3, o1, d0, y0, d1, attn, dq, dk, dv,
    y_in, up_in, down_in, sums, home, send, recv, local, near,
    up_s, up_r, down_s, down_r, y_s, y_r,
):
    me, blk = lax.axis_index("head"), lax.axis_index("blk")
    greet(nh, nblk, whole, me, blk)
    grads = (d0, d1)
    rows = attn.shape[0]
    group = nh * rows
    half = o1.shape[1] // 2
    kw = dk.shape[1] // nh
    f32, bf16 = jnp.float32, jnp.bfloat16
    nz = nblk // LINE
    hi, lo = blk // LINE, lax.rem(blk, LINE)

    def part(n, row):
        if n < 2:
            return (
                o1.at[aligned(row, rows), pl.ds(n * half, half)],
                (attn, dq)[n].at[:, aligned(me * 2 + 1, half)],
            )
        return (
            home.at[aligned(row, rows), pl.ds((n - 2) * kw, kw)],
            (dk, dv)[n - 2].at[:, aligned(me, kw)],
        )

    def to_peer(n, m):
        peer = lax.rem(me + m, nh)
        src, dst = part(n, peer)
        return remote(src, dst, (send.at[n, m - 1], recv.at[n, m - 1]), (peer, blk))

    def own(n):
        src, dst = part(n, me)
        return pltpu.make_async_copy(src, dst, local.at[n])

    def brought(m, which):
        cols = pl.ds(which * half, half)
        src = o0.at[aligned(me, rows), cols] if m == 0 else (r1, r2, r3)[m - 1].at[:, cols]
        dst = (attn, dq)[which].at[:, aligned(lax.rem(me - m + nh, nh) * 2, half)]
        return pltpu.make_async_copy(src, dst, near.at[m, which])

    order = (2, 3, 1) if nh == 4 else tuple(range(1, nh))

    def across(z):
        return remote(
            d1.at[aligned(nz + z, group), :], y_in.at[z], (y_s.at[z], y_r.at[z]),
            (me, blk + 1 - 2 * lo),
        )

    def start_outs():
        for n in range(2):
            for m in order:
                to_peer(n, m).start()
            own(n).start()
        for m in range(nh):
            for which in range(2):
                brought(m, which).start()

    def up(z):
        return remote(sums.at[z], up_in.at[z], (up_s.at[z], up_r.at[z]), (me, blk + LINE))

    def down(z):
        return remote(
            sums.at[z], down_in.at[z], (down_s.at[z], down_r.at[z]), (me, blk - LINE)
        )

    def keep(z, value):
        for j in range(2):
            sums[z, j] = value[j].astype(bf16)

    def mine(z):
        at = pl.ds(z * group, group)
        return [
            d0[at, :].astype(f32) + y0[at, :].astype(f32),
            d1[at, :].astype(f32) + y_in[z].astype(f32),
        ]

    def with_in(value, arrived, z):
        return [value[j] + arrived[z, j].astype(f32) for j in range(2)]

    def finish(value):
        for j in range(2):
            for which in range(2):
                at = which * 2 + j
                home[:, at * HEAD_SIZE : (at + 1) * HEAD_SIZE] = value[j][
                    :, which * HEAD_SIZE : (which + 1) * HEAD_SIZE
                ].astype(bf16)

    if whole:
        far_first = sorted(range(nz), key=lambda z: -abs(2 * z - nz + 1))
        for z in far_first:
            across(z).start()
        start_outs()
        for z in far_first:
            across(z).wait_recv()

            @pl.when(hi < z)
            def _(z=z):
                @pl.when(hi == 0)
                def _():
                    keep(z, mine(z))

                @pl.when(hi > 0)
                def _():
                    up(z).wait_recv()
                    keep(z, with_in(mine(z), up_in, z))

                up(z).start()

            @pl.when(hi > z)
            def _(z=z):
                @pl.when(hi == nz - 1)
                def _():
                    keep(z, mine(z))

                @pl.when(hi < nz - 1)
                def _():
                    down(z).wait_recv()
                    keep(z, with_in(mine(z), down_in, z))

                down(z).start()

        for z in range(nz):
            @pl.when(hi == z)
            def _(z=z):
                value = mine(z)
                if z > 0:
                    up(z).wait_recv()
                    value = with_in(value, up_in, z)
                if z < nz - 1:
                    down(z).wait_recv()
                    value = with_in(value, down_in, z)
                finish(value)

    else:
        start_outs()
        finish([grads[j][...].astype(f32) for j in range(2)])
    for n in (2, 3):
        for m in order:
            to_peer(n, m).start()
        own(n).start()
    if whole:
        for z in range(nz):
            across(z).wait_send()
            pl.when(hi < z)(lambda z=z: up(z).wait_send())
            pl.when(hi > z)(lambda z=z: down(z).wait_send())
    for n in range(4):
        for m in order:
            to_peer(n, m).wait()
        own(n).wait()
    for m in range(nh):
        for which in range(2):
            brought(m, which).wait()


def permuted(block, axis, distance):
    size = lax.axis_size(axis)
    return lax.ppermute(block, axis, [(i, (i + distance) % size) for i in range(size)])


def swapped(block):
    return lax.ppermute(block, "blk", [(i, i ^ 1) for i in range(lax.axis_size("blk"))])


def body(query, key, value, output_gradient, pair_codes, pair_counts):
    rows = query.shape[0]
    nh = lax.axis_size("head")
    nblk = lax.axis_size("blk")
    codes, counts = pair_codes[0], pair_counts[0]
    nstep = codes.shape[0]
    whole = nblk == nstep
    nz = nblk // LINE
    group = nh * rows
    bf16 = jnp.bfloat16
    dma = pltpu.SemaphoreType.DMA
    anywhere = pl.BlockSpec(memory_space=pl.ANY)
    in_vmem = pl.BlockSpec(memory_space=pltpu.VMEM)
    width = query.shape[1] // KEY_VALUE_HEADS
    pair = 2 * HEAD_SIZE
    like = jax.ShapeDtypeStruct
    q0, g0, kv0, kv1 = pl.pallas_call(
        functools.partial(enter, nh, nblk, whole),
        out_shape=(
            like((group, width), bf16),
            like((group, width), bf16),
            like((group * (nblk if whole else 1), pair), bf16),
            like((group * (nz if whole else 1), pair), bf16),
        ),
        in_specs=[anywhere] * 4,
        out_specs=[anywhere] * 4,
        scratch_shapes=[
            dma((6, nh - 1)), dma((6, nh - 1)), dma((6,)),
            dma((2, nz)), dma((2, nz)), dma((2, nz)), dma((2, nz)),
            dma((2 * nz,)), dma((2 * nz,)),
        ],
        compiler_params=pltpu.CompilerParams(collective_id=0, has_side_effects=True),
    )(query, key, value, output_gradient)
    query, output_gradient, q0, g0, kv0, kv1 = lax.optimization_barrier(
        (query, output_gradient, q0, g0, kv0, kv1)
    )
    me = lax.axis_index("head")

    def second(m):
        at = (lax.rem(me + m, nh) * 2 + 1) * width
        return jnp.concatenate(
            [
                lax.dynamic_slice_in_dim(x, at, width, 1)
                for x in (query, output_gradient)
            ],
            axis=1,
        )

    if whole:
        kv1 = jnp.concatenate([kv1, swapped(kv1)], axis=0)
    else:
        kv0, kv1 = (
            jnp.concatenate(
                [kv] + [permuted(kv, "blk", nstep - i) for i in range(1, nstep)], axis=0
            )
            for kv in (kv0, kv1)
        )
    qg1 = jnp.concatenate(
        [second(0)] + [permuted(second(m), "head", m) for m in range(1, nh)], axis=0
    )
    start = lax.axis_index("blk") if whole else jnp.int32(0)
    base0 = jnp.stack([start, jnp.int32(0), jnp.int32(1)]).astype(jnp.int32)
    base1 = jnp.stack([start, me, jnp.int32(nh - 1)]).astype(jnp.int32)

    def returned(grad):
        if whole:
            return grad
        parts = grad.reshape(nstep, group, -1)
        total = parts[0].astype(jnp.float32)
        for i in range(1, nstep):
            total += permuted(parts[i], "blk", i - nstep).astype(jnp.float32)
        return total.astype(bf16)

    o0, d0 = attention(whole, base0, codes, counts, q0, g0, kv0)
    came = [
        permuted(
            lax.dynamic_slice_in_dim(o0, lax.rem(me + m, nh) * rows, rows, 0), "head", m
        )
        for m in range(1, nh)
    ]
    y0 = swapped(d0[nz * group :]) if whole else d0
    d0 = returned(d0)
    o1, d1 = attention(whole, base1, codes, counts, qg1, qg1, kv1)
    d1 = returned(d1)
    y0 = y0 if whole else d0
    y_slots = (nz if whole else 1, group, pair)
    slots = (nz if whole else 1, 2, group, pair)
    return pl.pallas_call(
        functools.partial(leave, nh, nblk, whole),
        out_shape=(
            like(query.shape, bf16), like(query.shape, bf16),
            like(key.shape, bf16), like(value.shape, bf16),
        ),
        in_specs=[anywhere] * 5 + [in_vmem] * 3,
        out_specs=[anywhere] * 4,
        scratch_shapes=[
            pltpu.VMEM(y_slots, bf16), pltpu.VMEM(slots, bf16), pltpu.VMEM(slots, bf16),
            pltpu.VMEM(slots, bf16), pltpu.VMEM((group, 2 * pair), bf16),
            dma((4, nh - 1)), dma((4, nh - 1)), dma((4,)), dma((nh, 2)),
            dma((nz,)), dma((nz,)), dma((nz,)), dma((nz,)),
            dma((nz,)), dma((nz,)),
        ],
        compiler_params=pltpu.CompilerParams(
            collective_id=1, has_side_effects=True, vmem_limit_bytes=40 * 2**20
        ),
    )(o0, *came, o1, d0, y0, d1)


def solution(mesh):
    tokens = P(("blk", "head"), None)
    return jax.shard_map(
        body,
        mesh=mesh,
        in_specs=(tokens,) * 4 + (P("blk", None, None), P("blk", None)),
        out_specs=(tokens,) * 4,
        check_vma=False,
    )
```

```python
import functools
import math

import jax
import jax.numpy as jnp
from jax import lax
from jax.experimental import pallas as pl
from jax.experimental.pallas import tpu as pltpu
from jax.sharding import PartitionSpec as P

QUERY_HEADS = 64
KEY_VALUE_HEADS = 8
HEAD_SIZE = 128
BLOCK = 128
NEGATIVE_FILL = -1e30

NT = (((1,), (1,)), ((), ()))
NN = (((1,), (0,)), ((), ()))
TN = (((0,), (0,)), ((), ()))
MESH = pl.DeviceIdType.MESH
LINE = 2


def dot(a, b, dims):
    return lax.dot_general(a, b, dims, preferred_element_type=jnp.float32)


def query_block(nblocks, base_ref, turn):
    return lax.rem(base_ref[1] + base_ref[2] * turn, nblocks)


def attend(
    nstep, nblocks, heads, split, inputs, base_ref, codes_ref, counts_ref, *refs
):
    asked, (k_ref, v_ref, out_ref) = refs[:inputs], refs[inputs : inputs + 3]
    shares = 2 if split else 1
    dkv_refs = refs[inputs + 3 : inputs + 3 + shares]
    lst, cnt, qs, gs, scores, out_t, dq_t, dk, dv = refs[inputs + 3 + shares :]

    def place_of(base, s):
        at = lax.rem(base - s + nstep, nstep)
        if not split:
            return at
        far = lax.rem(at + base, LINE)
        return at // LINE + far * (nstep // LINE)

    scale = HEAD_SIZE ** (-0.5)
    c2 = scale * math.log2(math.e)
    turn = pl.program_id(0)
    qb = query_block(nblocks, base_ref, turn)
    width = heads * BLOCK
    room = nstep * nblocks
    both = 2 * BLOCK
    f32, bf16 = jnp.float32, jnp.bfloat16

    @pl.when(turn == 0)
    def _():
        dk[...] = jnp.zeros_like(dk)
        dv[...] = jnp.zeros_like(dv)
        base = base_ref[0]
        for b in range(nblocks):
            cnt[b] = 1
            lst[b * room] = place_of(base, 0) * nblocks + b

        def over_steps(s, _):
            place = place_of(base, s) * nblocks

            def over_codes(i, _):
                code = codes_ref[s, i]
                row = code // nblocks
                col = code - row * nblocks

                @pl.when(jnp.logical_or(s != 0, row != col))
                def _():
                    n = cnt[row]
                    lst[row * room + n] = place + col
                    cnt[row] = n + 1

                return 0

            return lax.fori_loop(0, counts_ref[s], over_codes, 0)

        lax.fori_loop(0, nstep, over_steps, 0)

    n = cnt[qb]
    first = qb * room
    chunks = (n + 1) // 2

    def rows_of(i):
        at = lst[first + jnp.where(i < n, i, 0)]
        return pl.ds(pl.multiple_of(at * BLOCK, BLOCK), BLOCK)

    def two(ref, c):
        return jnp.concatenate([ref[rows_of(2 * c), :], ref[rows_of(2 * c + 1), :]], axis=0)

    def turned(x):
        return jnp.transpose(x.astype(f32)).astype(bf16)

    def load(q_ref, g_ref, g_at):
        for h in range(heads):
            cols = slice(h * BLOCK, (h + 1) * BLOCK)
            qs[cols, :] = q_ref[:, cols]
            gs[cols, :] = g_ref[:, g_at + h * BLOCK : g_at + (h + 1) * BLOCK]

    if inputs == 2:
        load(asked[0], asked[1], 0)
    else:
        for m in range(inputs):
            pl.when(turn == m)(functools.partial(load, asked[m], asked[m], width))

    tiles = [slice(t * both, (t + 1) * both) for t in range(width // both)]

    def tile_top(s, cols, c, top):
        scores[c, :, cols] = s
        return jnp.maximum(top, jnp.max(s, axis=0, keepdims=True))

    def ending(s, c):
        last = jnp.where(2 * c + 1 < n, s[BLOCK:], NEGATIVE_FILL)
        return jnp.concatenate([s[:BLOCK], last], axis=0)

    key_at = lax.broadcasted_iota(jnp.int32, (both, both), 0)
    query_at = lax.broadcasted_iota(jnp.int32, (both, both), 1) % BLOCK
    seen = jnp.logical_or(key_at <= query_at, key_at >= BLOCK)
    kk = two(k_ref, 0)
    tops = []
    for cols in tiles:
        s = jnp.where(seen, dot(kk, qs[cols, :], NT), NEGATIVE_FILL)
        tops.append(tile_top(ending(s, 0), cols, 0, jnp.full((1, both), NEGATIVE_FILL, f32)))

    def score_pass(c, tops):
        kk = two(k_ref, c)
        return tuple(
            tile_top(ending(dot(kk, qs[cols, :], NT), c), cols, c, top)
            for cols, top in zip(tiles, tops)
        )

    tops = lax.fori_loop(1, chunks, score_pass, tuple(tops))
    out_t[...] = jnp.zeros_like(out_t)

    def weight_pass(c, totals):
        vt = turned(two(v_ref, c))
        new = []
        for cols, top, total in zip(tiles, tops, totals):
            w = jnp.exp2((scores[c, :, cols] - top) * c2)
            scores[c, :, cols] = w
            out_t[:, cols] += dot(vt, w.astype(bf16), NN)
            new.append(total + jnp.sum(w, axis=0, keepdims=True))
        return tuple(new)

    zero = tuple(jnp.zeros((1, both), f32) for _ in tiles)
    totals = lax.fori_loop(0, chunks, weight_pass, zero)
    invs = [1.0 / total for total in totals]

    row_dots = []
    for h in range(heads):
        cols = slice(h * BLOCK, (h + 1) * BLOCK)
        inv = invs[h // 2][:, (h % 2) * BLOCK : (h % 2 + 1) * BLOCK]
        attn = jnp.transpose(out_t[:, cols] * inv).astype(bf16)
        out_ref[:, cols] = attn
        prod = attn.astype(f32) * gs[cols, :].astype(f32)
        row_dots.append(jnp.sum(jnp.transpose(prod), axis=0, keepdims=True))
    row_dots = [
        jnp.concatenate(row_dots[2 * t : 2 * t + 2], axis=1) for t in range(len(tiles))
    ]
    dq_t[...] = jnp.zeros_like(dq_t)

    def grad_pass(c, _):
        kt = turned(two(k_ref, c))
        vv = two(v_ref, c)
        dv_now = jnp.zeros((both, HEAD_SIZE), f32)
        dk_now = jnp.zeros((both, HEAD_SIZE), f32)
        for cols, inv, row_dot in zip(tiles, invs, row_dots):
            p = scores[c, :, cols] * inv
            dv_now += dot(p.astype(bf16), gs[cols, :], NN)
            dp = dot(vv, gs[cols, :], NT)
            ds = (p * (dp - row_dot)).astype(bf16)
            dk_now += dot(ds, qs[cols, :], NN)
            dq_t[:, cols] += dot(kt, ds, NN)
        for i in range(2):
            rows = rows_of(2 * c + i)
            part = slice(i * BLOCK, (i + 1) * BLOCK)
            dv[rows, :] += dv_now[part]
            dk[rows, :] += dk_now[part]
        return 0

    lax.fori_loop(0, chunks, grad_pass, 0)
    for h in range(heads):
        cols = slice(h * BLOCK, (h + 1) * BLOCK)
        out_ref[:, width + h * BLOCK : width + (h + 1) * BLOCK] = jnp.transpose(
            dq_t[:, cols] * scale
        ).astype(bf16)

    @pl.when(turn == nblocks - 1)
    def _():
        for share, ref in enumerate(dkv_refs):
            rows = slice(share * ref.shape[0], (share + 1) * ref.shape[0])
            ref[:, :HEAD_SIZE] = (dk[rows, :] * scale).astype(bf16)
            ref[:, HEAD_SIZE:] = dv[rows, :].astype(bf16)


def attention(split, base, codes, counts, asked, kv):
    nstep = codes.shape[0]
    inputs = len(asked)
    width = HEAD_SIZE * (QUERY_HEADS // KEY_VALUE_HEADS)
    heads = width // HEAD_SIZE
    rows = asked[0].shape[0] * (1 if inputs == 2 else inputs)
    nblocks = rows // BLOCK
    keys = kv.shape[0]
    shares = 2 if split else 1
    f32, bf16 = jnp.float32, jnp.bfloat16
    flops = 6 * 2 * 30 * width * BLOCK * HEAD_SIZE
    whole_block = lambda i, *_: (0, 0)
    if inputs == 2:
        q_specs = [pl.BlockSpec((BLOCK, width), lambda i, *_: (i, 0))] * 2
    else:
        q_specs = [pl.BlockSpec((BLOCK, 2 * width), whole_block)] * inputs
    return pl.pallas_call(
        functools.partial(attend, nstep, nblocks, heads, split, inputs),
        out_shape=[jax.ShapeDtypeStruct((rows, 2 * width), bf16)]
        + [jax.ShapeDtypeStruct((keys // shares, 2 * HEAD_SIZE), bf16)] * shares,
        grid_spec=pltpu.PrefetchScalarGridSpec(
            num_scalar_prefetch=3,
            grid=(nblocks,),
            in_specs=q_specs
            + [
                pl.BlockSpec((keys, HEAD_SIZE), whole_block),
                pl.BlockSpec((keys, HEAD_SIZE), lambda i, *_: (0, 1)),
            ],
            out_specs=[
                pl.BlockSpec(
                    (BLOCK, 2 * width),
                    lambda i, base, *_: (query_block(nblocks, base, i), 0),
                ),
            ]
            + [pl.BlockSpec((keys // shares, 2 * HEAD_SIZE), whole_block)] * shares,
            scratch_shapes=[
                pltpu.SMEM((nblocks * nstep * nblocks,), jnp.int32),
                pltpu.SMEM((nblocks,), jnp.int32),
                pltpu.VMEM((width, HEAD_SIZE), bf16),
                pltpu.VMEM((width, HEAD_SIZE), bf16),
                pltpu.VMEM((nstep * nblocks // 2, 2 * BLOCK, width), f32),
                pltpu.VMEM((HEAD_SIZE, width), f32),
                pltpu.VMEM((HEAD_SIZE, width), f32),
                pltpu.VMEM((keys, HEAD_SIZE), f32),
                pltpu.VMEM((keys, HEAD_SIZE), f32),
            ],
        ),
        compiler_params=pltpu.CompilerParams(vmem_limit_bytes=48 * 2**20),
        cost_estimate=pl.CostEstimate(
            flops=16 * flops, bytes_accessed=2**23, transcendentals=30 * width * BLOCK
        ),
    )(base, codes, counts, *asked, kv, kv)


def greet(nh, nblk, whole, me, blk):
    barrier = pltpu.get_barrier_semaphore()
    for m in range(1, nh):
        pl.semaphore_signal(
            barrier, inc=1, device_id=(lax.rem(me + m, nh), blk), device_id_type=MESH
        )
    others = nblk if whole else 1
    for m in range(1, others):
        pl.semaphore_signal(
            barrier, inc=1, device_id=(me, lax.rem(blk + m, nblk)), device_id_type=MESH
        )
    pl.semaphore_wait(barrier, nh - 1 + others - 1)


def aligned(index, size):
    return pl.ds(pl.multiple_of(index * size, size), size)


def remote(src, dst, sems, device):
    return pltpu.make_async_remote_copy(
        src_ref=src, dst_ref=dst, send_sem=sems[0], recv_sem=sems[1],
        device_id=device, device_id_type=MESH,
    )


def enter(
    nh, nblk, whole, q, k, v, g, q0, g0, kv0, kv1, *refs
):
    cuts = refs[:nh]
    send, recv, local, near, up_s, up_r, down_s, down_r, y_s, y_r = refs[nh:]
    me, blk = lax.axis_index("head"), lax.axis_index("blk")
    greet(nh, nblk, whole, me, blk)
    rows = q.shape[0]
    qc = q0.shape[1]
    group = nh * rows
    nz = nblk // LINE
    hi, lo = blk // LINE, lax.rem(blk, LINE)
    keys = (kv0, kv1)

    def parts(n):
        if n < 4:
            j, which = n // 2, n % 2
            at = aligned((hi * nh if whole else 0) + me, rows)
            dst = keys[j].at[at, pl.ds(which * HEAD_SIZE, HEAD_SIZE)]
            return (k, v)[which], HEAD_SIZE, j, dst
        return (q, g)[n - 4], qc, 0, (q0, g0)[n - 4].at[aligned(me, rows), :]

    def to_peer(n, m):
        src, cols, j, dst = parts(n)
        peer = lax.rem(me + m, nh)
        return remote(
            src.at[:, aligned(peer * 2 + j, cols)], dst,
            (send.at[n, m - 1], recv.at[n, m - 1]), (peer, blk),
        )

    def own(n):
        src, cols, j, dst = parts(n)
        return pltpu.make_async_copy(src.at[:, aligned(me * 2 + j, cols)], dst, local.at[n])

    order = (2, 3, 1) if nh == 4 else tuple(range(1, nh))

    def start(n):
        for m in order:
            to_peer(n, m).start()
        own(n).start()

    def arrived(n):
        for m in order:
            to_peer(n, m).wait_recv()
        own(n).wait()

    def block(j, z):
        return keys[j].at[aligned(z, group), :]

    def up(j, d):
        return remote(
            block(j, hi - d), block(j, hi - d), (up_s.at[j, d], up_r.at[j, d]),
            (me, blk + LINE),
        )

    def down(j, d):
        return remote(
            block(j, hi + d), block(j, hi + d), (down_s.at[j, d], down_r.at[j, d]),
            (me, blk - LINE),
        )

    def across(z, slot):
        return remote(
            block(0, z), block(0, nz + z), (y_s.at[slot], y_r.at[slot]),
            (me, blk + 1 - 2 * lo),
        )

    def pass_on(j, d):
        if d > 0:
            pl.when(hi - d >= 0)(lambda: up(j, d - 1).wait_recv())
        if d < nz - 1:
            pl.when(jnp.logical_and(hi - d >= 0, hi < nz - 1))(lambda: up(j, d).start())
        if d > 0:
            pl.when(hi + d < nz)(lambda: down(j, d - 1).wait_recv())
        if d < nz - 1:
            pl.when(jnp.logical_and(hi + d < nz, hi > 0))(lambda: down(j, d).start())
        if j > 0:
            return
        if d == 0:
            across(hi, 0).start()
        else:
            pl.when(hi - d >= 0)(lambda: across(hi - d, d).start())
            pl.when(hi + d < nz)(lambda: across(hi + d, nz - 1 + d).start())

    for n in range(4):
        start(n)
    for j in range(2):
        arrived(2 * j)
        arrived(2 * j + 1)
        if whole:
            pass_on(j, 0)
    start(4)
    start(5)

    def cut(m, which):
        at = aligned(lax.rem(me + m, nh) * 2 + 1, qc)
        return pltpu.make_async_copy(
            (q, g)[which].at[:, at], cuts[m].at[:, pl.ds(which * qc, qc)], near.at[m, which]
        )

    for m in range(nh):
        for which in range(2):
            cut(m, which).start()
    if whole:
        for d in range(1, nz):
            pass_on(0, d)
            pass_on(1, d)
        across(hi, 0).wait()
        for d in range(1, nz):
            pl.when(hi - d >= 0)(lambda d=d: across(hi - d, d).wait())
            pl.when(hi + d < nz)(lambda d=d: across(hi + d, nz - 1 + d).wait())
        for j in range(2):
            for d in range(nz - 1):
                pl.when(jnp.logical_and(hi - d >= 0, hi < nz - 1))(
                    lambda j=j, d=d: up(j, d).wait_send()
                )
                pl.when(jnp.logical_and(hi + d < nz, hi > 0))(
                    lambda j=j, d=d: down(j, d).wait_send()
                )
    for m in range(nh):
        for which in range(2):
            cut(m, which).wait()
    arrived(4)
    arrived(5)
    for n in range(6):
        for m in order:
            to_peer(n, m).wait_send()


def leave(
    nh, nblk, whole, o0, r1, r2, r3, o1, d0, y0, d1, far, attn, dq, dk, dv,
    y_in, up_in, down_in, sums, home, send, recv, local, near,
    up_s, up_r, down_s, down_r, y_s, y_r,
):
    me, blk = lax.axis_index("head"), lax.axis_index("blk")
    greet(nh, nblk, whole, me, blk)
    grads = (d0, d1)
    rows = attn.shape[0]
    group = nh * rows
    half = o1.shape[1] // 2
    kw = dk.shape[1] // nh
    f32, bf16 = jnp.float32, jnp.bfloat16
    nz = nblk // LINE
    hi, lo = blk // LINE, lax.rem(blk, LINE)

    def part(n, row):
        if n < 2:
            return (
                o1.at[aligned(row, rows), pl.ds(n * half, half)],
                (attn, dq)[n].at[:, aligned(me * 2 + 1, half)],
            )
        return (
            home.at[aligned(row, rows), pl.ds((n - 2) * kw, kw)],
            (dk, dv)[n - 2].at[:, aligned(me, kw)],
        )

    def to_peer(n, m):
        peer = lax.rem(me + m, nh)
        src, dst = part(n, peer)
        return remote(src, dst, (send.at[n, m - 1], recv.at[n, m - 1]), (peer, blk))

    def own(n):
        src, dst = part(n, me)
        return pltpu.make_async_copy(src, dst, local.at[n])

    def brought(m, which):
        cols = pl.ds(which * half, half)
        src = o0.at[aligned(me, rows), cols] if m == 0 else (r1, r2, r3)[m - 1].at[:, cols]
        dst = (attn, dq)[which].at[:, aligned(lax.rem(me - m + nh, nh) * 2, half)]
        return pltpu.make_async_copy(src, dst, near.at[m, which])

    order = (2, 3, 1) if nh == 4 else tuple(range(1, nh))

    def across(z):
        return remote(
            far.at[pl.ds(z * group, group), :], y_in.at[z], (y_s.at[z], y_r.at[z]),
            (me, blk + 1 - 2 * lo),
        )

    def start_outs():
        for n in range(2):
            for m in order:
                to_peer(n, m).start()
            own(n).start()
        for m in range(nh):
            for which in range(2):
                brought(m, which).start()

    def up(z, j):
        return remote(
            sums.at[z, j], up_in.at[z, j], (up_s.at[z, j], up_r.at[z, j]), (me, blk + LINE)
        )

    def down(z, j):
        return remote(
            sums.at[z, j], down_in.at[z, j], (down_s.at[z, j], down_r.at[z, j]),
            (me, blk - LINE),
        )

    def mine(z, j):
        at = pl.ds(z * group, group)
        came = y0[at, :] if j == 0 else y_in[z]
        return grads[j][at, :].astype(f32) + came.astype(f32)

    def finish(j, value):
        for which in range(2):
            at = which * 2 + j
            home[:, at * HEAD_SIZE : (at + 1) * HEAD_SIZE] = value[
                :, which * HEAD_SIZE : (which + 1) * HEAD_SIZE
            ].astype(bf16)

    def hop(z, j, copy, first, arrivals):
        @pl.when(hi == first)
        def _():
            sums[z, j] = mine(z, j).astype(bf16)

        @pl.when(hi != first)
        def _():
            copy(z, j).wait_recv()
            sums[z, j] = (mine(z, j) + arrivals[z, j].astype(f32)).astype(bf16)

        copy(z, j).start()

    if whole:
        far_first = sorted(range(nz), key=lambda z: -abs(2 * z - nz + 1))
        for z in far_first:
            across(z).start()
        start_outs()
        for j in range(2):
            for z in far_first:
                if j == 1:
                    across(z).wait_recv()
                pl.when(hi < z)(functools.partial(hop, z, j, up, 0, up_in))
                pl.when(hi > z)(functools.partial(hop, z, j, down, nz - 1, down_in))
        for j in range(2):
            for z in range(nz):
                @pl.when(hi == z)
                def _(z=z, j=j):
                    value = mine(z, j)
                    if z > 0:
                        up(z, j).wait_recv()
                        value += up_in[z, j].astype(f32)
                    if z < nz - 1:
                        down(z, j).wait_recv()
                        value += down_in[z, j].astype(f32)
                    finish(j, value)

    else:
        start_outs()
        for j in range(2):
            finish(j, grads[j][...].astype(f32))
    for n in (2, 3):
        for m in order:
            to_peer(n, m).start()
        own(n).start()
    if whole:
        for z in range(nz):
            across(z).wait_send()
            for j in range(2):
                pl.when(hi < z)(lambda z=z, j=j: up(z, j).wait_send())
                pl.when(hi > z)(lambda z=z, j=j: down(z, j).wait_send())
    for n in range(4):
        for m in order:
            to_peer(n, m).wait()
        own(n).wait()
    for m in range(nh):
        for which in range(2):
            brought(m, which).wait()


def permuted(block, axis, distance):
    size = lax.axis_size(axis)
    return lax.ppermute(block, axis, [(i, (i + distance) % size) for i in range(size)])


def swapped(block):
    return lax.ppermute(block, "blk", [(i, i ^ 1) for i in range(lax.axis_size("blk"))])


def body(query, key, value, output_gradient, pair_codes, pair_counts):
    rows = query.shape[0]
    nh = lax.axis_size("head")
    nblk = lax.axis_size("blk")
    codes, counts = pair_codes[0], pair_counts[0]
    nstep = codes.shape[0]
    whole = nblk == nstep
    nz = nblk // LINE
    group = nh * rows
    bf16 = jnp.bfloat16
    dma = pltpu.SemaphoreType.DMA
    anywhere = pl.BlockSpec(memory_space=pl.ANY)
    in_vmem = pl.BlockSpec(memory_space=pltpu.VMEM)
    width = query.shape[1] // KEY_VALUE_HEADS
    pair = 2 * HEAD_SIZE
    like = jax.ShapeDtypeStruct
    q0, g0, kv0, kv1, *cuts = pl.pallas_call(
        functools.partial(enter, nh, nblk, whole),
        out_shape=(
            like((group, width), bf16),
            like((group, width), bf16),
            like((group * (nblk if whole else 1), pair), bf16),
            like((group * (nz if whole else 1), pair), bf16),
        )
        + (like((rows, 2 * width), bf16),) * nh,
        in_specs=[anywhere] * 4,
        out_specs=[anywhere] * (4 + nh),
        scratch_shapes=[
            dma((6, nh - 1)), dma((6, nh - 1)), dma((6,)), dma((nh, 2)),
            dma((2, nz)), dma((2, nz)), dma((2, nz)), dma((2, nz)),
            dma((2 * nz,)), dma((2 * nz,)),
        ],
        compiler_params=pltpu.CompilerParams(collective_id=0, has_side_effects=True),
    )(query, key, value, output_gradient)
    me = lax.axis_index("head")
    if whole:
        kv1 = jnp.concatenate([kv1, swapped(kv1)], axis=0)
    else:
        kv0, kv1 = (
            jnp.concatenate(
                [kv] + [permuted(kv, "blk", nstep - i) for i in range(1, nstep)], axis=0
            )
            for kv in (kv0, kv1)
        )
    qg1 = [cuts[0]] + [permuted(cuts[m], "head", m) for m in range(1, nh)]
    start = lax.axis_index("blk") if whole else jnp.int32(0)
    base0 = jnp.stack([start, jnp.int32(0), jnp.int32(1)]).astype(jnp.int32)
    base1 = jnp.stack([start, me, jnp.int32(nh - 1)]).astype(jnp.int32)

    def returned(grad):
        if whole:
            return grad
        parts = grad.reshape(nstep, group, -1)
        total = parts[0].astype(jnp.float32)
        for i in range(1, nstep):
            total += permuted(parts[i], "blk", i - nstep).astype(jnp.float32)
        return total.astype(bf16)

    o0, *d0 = attention(whole, base0, codes, counts, [q0, g0], kv0)
    came = [
        permuted(
            lax.dynamic_slice_in_dim(o0, lax.rem(me + m, nh) * rows, rows, 0), "head", m
        )
        for m in range(1, nh)
    ]
    y0 = swapped(d0[1]) if whole else returned(d0[0])
    o1, *d1 = attention(whole, base1, codes, counts, qg1, kv1)
    if not whole:
        d0, d1 = [y0], [returned(d1[0])]
    y_slots = (nz if whole else 1, group, pair)
    slots = (nz if whole else 1, 2, group, pair)
    return pl.pallas_call(
        functools.partial(leave, nh, nblk, whole),
        out_shape=(
            like(query.shape, bf16), like(query.shape, bf16),
            like(key.shape, bf16), like(value.shape, bf16),
        ),
        in_specs=[anywhere] * 5 + [in_vmem] * 4,
        out_specs=[anywhere] * 4,
        scratch_shapes=[
            pltpu.VMEM(y_slots, bf16), pltpu.VMEM(slots, bf16), pltpu.VMEM(slots, bf16),
            pltpu.VMEM(slots, bf16), pltpu.VMEM((group, 2 * pair), bf16),
            dma((4, nh - 1)), dma((4, nh - 1)), dma((4,)), dma((nh, 2)),
            dma((nz, 2)), dma((nz, 2)), dma((nz, 2)), dma((nz, 2)),
            dma((nz,)), dma((nz,)),
        ],
        compiler_params=pltpu.CompilerParams(
            collective_id=1, has_side_effects=True, vmem_limit_bytes=40 * 2**20
        ),
    )(o0, *came, o1, d0[0], y0, d1[0], d1[-1])


def solution(mesh):
    tokens = P(("blk", "head"), None)
    return jax.shard_map(
        body,
        mesh=mesh,
        in_specs=(tokens,) * 4 + (P("blk", None, None), P("blk", None)),
        out_specs=(tokens,) * 4,
        check_vma=False,
    )
```

```python
import functools
import math

import jax
import jax.numpy as jnp
from jax import lax
from jax.experimental import pallas as pl
from jax.experimental.pallas import tpu as pltpu
from jax.sharding import PartitionSpec as P

QUERY_HEADS = 64
KEY_VALUE_HEADS = 8
HEAD_SIZE = 128
BLOCK = 128
NEGATIVE_FILL = -1e30

NT = (((1,), (1,)), ((), ()))
NN = (((1,), (0,)), ((), ()))
TN = (((0,), (0,)), ((), ()))
MESH = pl.DeviceIdType.MESH
LINE = 2


def dot(a, b, dims):
    return lax.dot_general(a, b, dims, preferred_element_type=jnp.float32)


def query_block(nblocks, base_ref, turn):
    return lax.rem(base_ref[1] + base_ref[2] * turn, nblocks)


def attend(
    nstep, nblocks, heads, split, inputs, base_ref, codes_ref, counts_ref, *refs
):
    asked, (k_ref, v_ref, out_ref) = refs[:inputs], refs[inputs : inputs + 3]
    shares = 2 if split else 1
    dkv_refs = refs[inputs + 3 : inputs + 3 + shares]
    lst, cnt, qs, gs, scores, out_t, dq_t, dk, dv = refs[inputs + 3 + shares :]

    def place_of(base, s):
        at = lax.rem(base - s + nstep, nstep)
        if not split:
            return at
        far = lax.rem(at + base, LINE)
        return at // LINE + far * (nstep // LINE)

    scale = HEAD_SIZE ** (-0.5)
    c2 = scale * math.log2(math.e)
    turn = pl.program_id(0)
    qb = query_block(nblocks, base_ref, turn)
    width = heads * BLOCK
    room = nstep * nblocks
    both = 2 * BLOCK
    f32, bf16 = jnp.float32, jnp.bfloat16

    @pl.when(turn == 0)
    def _():
        dk[...] = jnp.zeros_like(dk)
        dv[...] = jnp.zeros_like(dv)
        base = base_ref[0]
        for b in range(nblocks):
            cnt[b] = 1
            lst[b * room] = place_of(base, 0) * nblocks + b

        def over_steps(s, _):
            place = place_of(base, s) * nblocks

            def over_codes(i, _):
                code = codes_ref[s, i]
                row = code // nblocks
                col = code - row * nblocks

                @pl.when(jnp.logical_or(s != 0, row != col))
                def _():
                    n = cnt[row]
                    lst[row * room + n] = place + col
                    cnt[row] = n + 1

                return 0

            return lax.fori_loop(0, counts_ref[s], over_codes, 0)

        lax.fori_loop(0, nstep, over_steps, 0)

    n = cnt[qb]
    first = qb * room
    chunks = (n + 1) // 2

    def rows_of(i):
        at = lst[first + jnp.where(i < n, i, 0)]
        return pl.ds(pl.multiple_of(at * BLOCK, BLOCK), BLOCK)

    def two(ref, c):
        return jnp.concatenate([ref[rows_of(2 * c), :], ref[rows_of(2 * c + 1), :]], axis=0)

    def turned(x):
        return jnp.transpose(x.astype(f32)).astype(bf16)

    def load(q_ref, g_ref, g_at):
        for h in range(heads):
            cols = slice(h * BLOCK, (h + 1) * BLOCK)
            qs[cols, :] = q_ref[:, cols]
            gs[cols, :] = g_ref[:, g_at + h * BLOCK : g_at + (h + 1) * BLOCK]

    if inputs == 2:
        load(asked[0], asked[1], 0)
    else:
        for m in range(inputs):
            pl.when(turn == m)(functools.partial(load, asked[m], asked[m], width))

    tiles = [slice(t * both, (t + 1) * both) for t in range(width // both)]

    def tile_top(s, cols, c, top):
        scores[c, :, cols] = s
        return jnp.maximum(top, jnp.max(s, axis=0, keepdims=True))

    def ending(s, c):
        last = jnp.where(2 * c + 1 < n, s[BLOCK:], NEGATIVE_FILL)
        return jnp.concatenate([s[:BLOCK], last], axis=0)

    key_at = lax.broadcasted_iota(jnp.int32, (both, both), 0)
    query_at = lax.broadcasted_iota(jnp.int32, (both, both), 1) % BLOCK
    seen = jnp.logical_or(key_at <= query_at, key_at >= BLOCK)
    kk = two(k_ref, 0)
    tops = []
    for cols in tiles:
        s = jnp.where(seen, dot(kk, qs[cols, :], NT), NEGATIVE_FILL)
        tops.append(tile_top(ending(s, 0), cols, 0, jnp.full((1, both), NEGATIVE_FILL, f32)))

    def score_pass(c, tops):
        kk = two(k_ref, c)
        return tuple(
            tile_top(ending(dot(kk, qs[cols, :], NT), c), cols, c, top)
            for cols, top in zip(tiles, tops)
        )

    tops = lax.fori_loop(1, chunks, score_pass, tuple(tops))
    out_t[...] = jnp.zeros_like(out_t)

    def weight_pass(c, totals):
        vt = turned(two(v_ref, c))
        new = []
        for cols, top, total in zip(tiles, tops, totals):
            w = jnp.exp2((scores[c, :, cols] - top) * c2)
            scores[c, :, cols] = w
            out_t[:, cols] += dot(vt, w.astype(bf16), NN)
            new.append(total + jnp.sum(w, axis=0, keepdims=True))
        return tuple(new)

    zero = tuple(jnp.zeros((1, both), f32) for _ in tiles)
    totals = lax.fori_loop(0, chunks, weight_pass, zero)
    invs = [1.0 / total for total in totals]

    row_dots = []
    for h in range(heads):
        cols = slice(h * BLOCK, (h + 1) * BLOCK)
        inv = invs[h // 2][:, (h % 2) * BLOCK : (h % 2 + 1) * BLOCK]
        attn = jnp.transpose(out_t[:, cols] * inv).astype(bf16)
        out_ref[:, cols] = attn
        prod = attn.astype(f32) * gs[cols, :].astype(f32)
        row_dots.append(jnp.sum(jnp.transpose(prod), axis=0, keepdims=True))
    row_dots = [
        jnp.concatenate(row_dots[2 * t : 2 * t + 2], axis=1) for t in range(len(tiles))
    ]
    dq_t[...] = jnp.zeros_like(dq_t)

    def grad_pass(c, _):
        kt = turned(two(k_ref, c))
        vv = two(v_ref, c)
        dv_now = jnp.zeros((both, HEAD_SIZE), f32)
        dk_now = jnp.zeros((both, HEAD_SIZE), f32)
        for cols, inv, row_dot in zip(tiles, invs, row_dots):
            p = scores[c, :, cols] * inv
            dv_now += dot(p.astype(bf16), gs[cols, :], NN)
            dp = dot(vv, gs[cols, :], NT)
            ds = (p * (dp - row_dot)).astype(bf16)
            dk_now += dot(ds, qs[cols, :], NN)
            dq_t[:, cols] += dot(kt, ds, NN)
        for i in range(2):
            rows = rows_of(2 * c + i)
            part = slice(i * BLOCK, (i + 1) * BLOCK)
            dv[rows, :] += dv_now[part]
            dk[rows, :] += dk_now[part]
        return 0

    lax.fori_loop(0, chunks, grad_pass, 0)
    for h in range(heads):
        cols = slice(h * BLOCK, (h + 1) * BLOCK)
        out_ref[:, width + h * BLOCK : width + (h + 1) * BLOCK] = jnp.transpose(
            dq_t[:, cols] * scale
        ).astype(bf16)

    @pl.when(turn == nblocks - 1)
    def _():
        for share, ref in enumerate(dkv_refs):
            rows = slice(share * ref.shape[0], (share + 1) * ref.shape[0])
            ref[:, :HEAD_SIZE] = (dk[rows, :] * scale).astype(bf16)
            ref[:, HEAD_SIZE:] = dv[rows, :].astype(bf16)


def attention(split, base, codes, counts, asked, kv):
    nstep = codes.shape[0]
    inputs = len(asked)
    width = HEAD_SIZE * (QUERY_HEADS // KEY_VALUE_HEADS)
    heads = width // HEAD_SIZE
    rows = asked[0].shape[0] * (1 if inputs == 2 else inputs)
    nblocks = rows // BLOCK
    keys = kv.shape[0]
    shares = 2 if split else 1
    f32, bf16 = jnp.float32, jnp.bfloat16
    flops = 6 * 2 * 30 * width * BLOCK * HEAD_SIZE
    whole_block = lambda i, *_: (0, 0)
    if inputs == 2:
        q_specs = [pl.BlockSpec((BLOCK, width), lambda i, *_: (i, 0))] * 2
    else:
        q_specs = [pl.BlockSpec((BLOCK, 2 * width), whole_block)] * inputs
    return pl.pallas_call(
        functools.partial(attend, nstep, nblocks, heads, split, inputs),
        out_shape=[jax.ShapeDtypeStruct((rows, 2 * width), bf16)]
        + [jax.ShapeDtypeStruct((keys // shares, 2 * HEAD_SIZE), bf16)] * shares,
        grid_spec=pltpu.PrefetchScalarGridSpec(
            num_scalar_prefetch=3,
            grid=(nblocks,),
            in_specs=q_specs
            + [
                pl.BlockSpec((keys, HEAD_SIZE), whole_block),
                pl.BlockSpec((keys, HEAD_SIZE), lambda i, *_: (0, 1)),
            ],
            out_specs=[
                pl.BlockSpec(
                    (BLOCK, 2 * width),
                    lambda i, base, *_: (query_block(nblocks, base, i), 0),
                ),
            ]
            + [pl.BlockSpec((keys // shares, 2 * HEAD_SIZE), whole_block)] * shares,
            scratch_shapes=[
                pltpu.SMEM((nblocks * nstep * nblocks,), jnp.int32),
                pltpu.SMEM((nblocks,), jnp.int32),
                pltpu.VMEM((width, HEAD_SIZE), bf16),
                pltpu.VMEM((width, HEAD_SIZE), bf16),
                pltpu.VMEM((nstep * nblocks // 2, 2 * BLOCK, width), f32),
                pltpu.VMEM((HEAD_SIZE, width), f32),
                pltpu.VMEM((HEAD_SIZE, width), f32),
                pltpu.VMEM((keys, HEAD_SIZE), f32),
                pltpu.VMEM((keys, HEAD_SIZE), f32),
            ],
        ),
        compiler_params=pltpu.CompilerParams(vmem_limit_bytes=48 * 2**20),
        cost_estimate=pl.CostEstimate(
            flops=16 * flops, bytes_accessed=2**23, transcendentals=30 * width * BLOCK
        ),
    )(base, codes, counts, *asked, kv, kv)


def greet(nh, nblk, whole, me, blk):
    barrier = pltpu.get_barrier_semaphore()
    for m in range(1, nh):
        pl.semaphore_signal(
            barrier, inc=1, device_id=(lax.rem(me + m, nh), blk), device_id_type=MESH
        )
    others = nblk if whole else 1
    for m in range(1, others):
        pl.semaphore_signal(
            barrier, inc=1, device_id=(me, lax.rem(blk + m, nblk)), device_id_type=MESH
        )
    pl.semaphore_wait(barrier, nh - 1 + others - 1)


def aligned(index, size):
    return pl.ds(pl.multiple_of(index * size, size), size)


def remote(src, dst, sems, device):
    return pltpu.make_async_remote_copy(
        src_ref=src, dst_ref=dst, send_sem=sems[0], recv_sem=sems[1],
        device_id=device, device_id_type=MESH,
    )


def enter(
    nh, nblk, whole, q, k, v, g, q0, g0, kv0, kv1, *refs
):
    cuts = refs[:nh]
    send, recv, up_s, up_r, down_s, down_r, y_s, y_r = refs[nh:]
    me, blk = lax.axis_index("head"), lax.axis_index("blk")
    greet(nh, nblk, whole, me, blk)
    rows = q.shape[0]
    qc = q0.shape[1]
    group = nh * rows
    nz = nblk // LINE
    hi, lo = blk // LINE, lax.rem(blk, LINE)
    keys = (kv0, kv1)

    def parts(n):
        if n < 4:
            j, which = n // 2, n % 2
            at = aligned((hi * nh if whole else 0) + me, rows)
            dst = keys[j].at[at, pl.ds(which * HEAD_SIZE, HEAD_SIZE)]
            return (k, v)[which], HEAD_SIZE, j, dst
        return (q, g)[n - 4], qc, 0, (q0, g0)[n - 4].at[aligned(me, rows), :]

    def to_peer(n, m):
        src, cols, j, dst = parts(n)
        peer = lax.rem(me + m, nh)
        return remote(
            src.at[:, aligned(peer * 2 + j, cols)], dst,
            (send.at[n, m - 1], recv.at[n, m - 1]), (peer, blk),
        )

    def own(n):
        src, cols, j, dst = parts(n)
        dst[...] = src[:, aligned(me * 2 + j, cols)]

    order = (2, 3, 1) if nh == 4 else tuple(range(1, nh))

    def start(n):
        for m in order:
            to_peer(n, m).start()

    def arrived(n):
        for m in order:
            to_peer(n, m).wait_recv()

    def block(j, z):
        return keys[j].at[aligned(z, group), :]

    def up(j, d):
        return remote(
            block(j, hi - d), block(j, hi - d), (up_s.at[j, d], up_r.at[j, d]),
            (me, blk + LINE),
        )

    def down(j, d):
        return remote(
            block(j, hi + d), block(j, hi + d), (down_s.at[j, d], down_r.at[j, d]),
            (me, blk - LINE),
        )

    def across(z, slot):
        return remote(
            block(0, z), block(0, nz + z), (y_s.at[slot], y_r.at[slot]),
            (me, blk + 1 - 2 * lo),
        )

    def pass_on(j, d):
        if d > 0:
            pl.when(hi - d >= 0)(lambda: up(j, d - 1).wait_recv())
        if d < nz - 1:
            pl.when(jnp.logical_and(hi - d >= 0, hi < nz - 1))(lambda: up(j, d).start())
        if d > 0:
            pl.when(hi + d < nz)(lambda: down(j, d - 1).wait_recv())
        if d < nz - 1:
            pl.when(jnp.logical_and(hi + d < nz, hi > 0))(lambda: down(j, d).start())
        if j > 0:
            return
        if d == 0:
            across(hi, 0).start()
        else:
            pl.when(hi - d >= 0)(lambda: across(hi - d, d).start())
            pl.when(hi + d < nz)(lambda: across(hi + d, nz - 1 + d).start())

    for n in range(4):
        start(n)
    for n in range(4):
        own(n)
    for j in range(2):
        arrived(2 * j)
        arrived(2 * j + 1)
        if whole:
            pass_on(j, 0)
    start(4)
    start(5)

    own(4)
    own(5)
    for m in range(nh):
        at = aligned(lax.rem(me + m, nh) * 2 + 1, qc)
        cuts[m][:, :qc] = q[:, at]
        cuts[m][:, qc:] = g[:, at]
    if whole:
        for d in range(1, nz):
            pass_on(0, d)
            pass_on(1, d)
        across(hi, 0).wait()
        for d in range(1, nz):
            pl.when(hi - d >= 0)(lambda d=d: across(hi - d, d).wait())
            pl.when(hi + d < nz)(lambda d=d: across(hi + d, nz - 1 + d).wait())
        for j in range(2):
            for d in range(nz - 1):
                pl.when(jnp.logical_and(hi - d >= 0, hi < nz - 1))(
                    lambda j=j, d=d: up(j, d).wait_send()
                )
                pl.when(jnp.logical_and(hi + d < nz, hi > 0))(
                    lambda j=j, d=d: down(j, d).wait_send()
                )
    arrived(4)
    arrived(5)
    for n in range(6):
        for m in order:
            to_peer(n, m).wait_send()


def leave(
    nh, nblk, whole, o0, r1, r2, r3, o1, d0, y0, d1, far, attn, dq, dk, dv,
    y_in, up_in, down_in, sums, home, send, recv,
    up_s, up_r, down_s, down_r, y_s, y_r,
):
    me, blk = lax.axis_index("head"), lax.axis_index("blk")
    greet(nh, nblk, whole, me, blk)
    grads = (d0, d1)
    rows = attn.shape[0]
    group = nh * rows
    half = o1.shape[1] // 2
    kw = dk.shape[1] // nh
    f32, bf16 = jnp.float32, jnp.bfloat16
    nz = nblk // LINE
    hi, lo = blk // LINE, lax.rem(blk, LINE)

    def part(n, row):
        if n < 2:
            return (
                o1.at[aligned(row, rows), pl.ds(n * half, half)],
                (attn, dq)[n].at[:, aligned(me * 2 + 1, half)],
            )
        return (
            home.at[aligned(row, rows), pl.ds((n - 2) * kw, kw)],
            (dk, dv)[n - 2].at[:, aligned(me, kw)],
        )

    def to_peer(n, m):
        peer = lax.rem(me + m, nh)
        src, dst = part(n, peer)
        return remote(src, dst, (send.at[n, m - 1], recv.at[n, m - 1]), (peer, blk))

    def own(n):
        src, dst = part(n, me)
        dst[...] = src[...]

    def brought(m, which):
        cols = pl.ds(which * half, half)
        src = o0.at[aligned(me, rows), cols] if m == 0 else (r1, r2, r3)[m - 1].at[:, cols]
        to = aligned(lax.rem(me - m + nh, nh) * 2, half)
        (attn, dq)[which][:, to] = src[...]

    order = (2, 3, 1) if nh == 4 else tuple(range(1, nh))

    def across(z):
        return remote(
            far.at[pl.ds(z * group, group), :], y_in.at[z], (y_s.at[z], y_r.at[z]),
            (me, blk + 1 - 2 * lo),
        )

    def start_outs():
        for n in range(2):
            for m in order:
                to_peer(n, m).start()

    def bring_outs():
        for n in range(2):
            own(n)
        for m in range(nh):
            for which in range(2):
                brought(m, which)

    def up(z, j):
        return remote(
            sums.at[z, j], up_in.at[z, j], (up_s.at[z, j], up_r.at[z, j]), (me, blk + LINE)
        )

    def down(z, j):
        return remote(
            sums.at[z, j], down_in.at[z, j], (down_s.at[z, j], down_r.at[z, j]),
            (me, blk - LINE),
        )

    def mine(z, j):
        at = pl.ds(z * group, group)
        came = y0[at, :] if j == 0 else y_in[z]
        return grads[j][at, :].astype(f32) + came.astype(f32)

    def finish(j, value):
        for which in range(2):
            at = which * 2 + j
            home[:, at * HEAD_SIZE : (at + 1) * HEAD_SIZE] = value[
                :, which * HEAD_SIZE : (which + 1) * HEAD_SIZE
            ].astype(bf16)

    def hop(z, j, copy, first, arrivals):
        @pl.when(hi == first)
        def _():
            sums[z, j] = mine(z, j).astype(bf16)

        @pl.when(hi != first)
        def _():
            copy(z, j).wait_recv()
            sums[z, j] = (mine(z, j) + arrivals[z, j].astype(f32)).astype(bf16)

        copy(z, j).start()

    if whole:
        far_first = sorted(range(nz), key=lambda z: -abs(2 * z - nz + 1))
        for z in far_first:
            across(z).start()
        start_outs()
        for j in range(2):
            for z in far_first:
                if j == 1:
                    across(z).wait_recv()
                pl.when(hi < z)(functools.partial(hop, z, j, up, 0, up_in))
                pl.when(hi > z)(functools.partial(hop, z, j, down, nz - 1, down_in))
        for j in range(2):
            for z in range(nz):
                @pl.when(hi == z)
                def _(z=z, j=j):
                    value = mine(z, j)
                    if z > 0:
                        up(z, j).wait_recv()
                        value += up_in[z, j].astype(f32)
                    if z < nz - 1:
                        down(z, j).wait_recv()
                        value += down_in[z, j].astype(f32)
                    finish(j, value)

    else:
        start_outs()
        for j in range(2):
            finish(j, grads[j][...].astype(f32))
    for n in (2, 3):
        for m in order:
            to_peer(n, m).start()
        own(n)
    bring_outs()
    if whole:
        for z in range(nz):
            across(z).wait_send()
            for j in range(2):
                pl.when(hi < z)(lambda z=z, j=j: up(z, j).wait_send())
                pl.when(hi > z)(lambda z=z, j=j: down(z, j).wait_send())
    for n in range(4):
        for m in order:
            to_peer(n, m).wait()


def permuted(block, axis, distance):
    size = lax.axis_size(axis)
    return lax.ppermute(block, axis, [(i, (i + distance) % size) for i in range(size)])


def swapped(block):
    return lax.ppermute(block, "blk", [(i, i ^ 1) for i in range(lax.axis_size("blk"))])


def body(query, key, value, output_gradient, pair_codes, pair_counts):
    rows = query.shape[0]
    nh = lax.axis_size("head")
    nblk = lax.axis_size("blk")
    codes, counts = pair_codes[0], pair_counts[0]
    nstep = codes.shape[0]
    whole = nblk == nstep
    nz = nblk // LINE
    group = nh * rows
    bf16 = jnp.bfloat16
    dma = pltpu.SemaphoreType.DMA
    in_vmem = pl.BlockSpec(memory_space=pltpu.VMEM)
    width = query.shape[1] // KEY_VALUE_HEADS
    pair = 2 * HEAD_SIZE
    like = jax.ShapeDtypeStruct
    q0, g0, kv0, kv1, *cuts = pl.pallas_call(
        functools.partial(enter, nh, nblk, whole),
        out_shape=(
            like((group, width), bf16),
            like((group, width), bf16),
            like((group * (nblk if whole else 1), pair), bf16),
            like((group * (nz if whole else 1), pair), bf16),
        )
        + (like((rows, 2 * width), bf16),) * nh,
        in_specs=[in_vmem] * 4,
        out_specs=[in_vmem] * (4 + nh),
        scratch_shapes=[
            dma((6, nh - 1)), dma((6, nh - 1)),
            dma((2, nz)), dma((2, nz)), dma((2, nz)), dma((2, nz)),
            dma((2 * nz,)), dma((2 * nz,)),
        ],
        compiler_params=pltpu.CompilerParams(
            collective_id=0, has_side_effects=True, vmem_limit_bytes=40 * 2**20
        ),
    )(query, key, value, output_gradient)
    me = lax.axis_index("head")
    if whole:
        kv1 = jnp.concatenate([kv1, swapped(kv1)], axis=0)
    else:
        kv0, kv1 = (
            jnp.concatenate(
                [kv] + [permuted(kv, "blk", nstep - i) for i in range(1, nstep)], axis=0
            )
            for kv in (kv0, kv1)
        )
    qg1 = [cuts[0]] + [permuted(cuts[m], "head", m) for m in range(1, nh)]
    start = lax.axis_index("blk") if whole else jnp.int32(0)
    base0 = jnp.stack([start, jnp.int32(0), jnp.int32(1)]).astype(jnp.int32)
    base1 = jnp.stack([start, me, jnp.int32(nh - 1)]).astype(jnp.int32)

    def returned(grad):
        if whole:
            return grad
        parts = grad.reshape(nstep, group, -1)
        total = parts[0].astype(jnp.float32)
        for i in range(1, nstep):
            total += permuted(parts[i], "blk", i - nstep).astype(jnp.float32)
        return total.astype(bf16)

    o0, *d0 = attention(whole, base0, codes, counts, [q0, g0], kv0)
    came = [
        permuted(
            lax.dynamic_slice_in_dim(o0, lax.rem(me + m, nh) * rows, rows, 0), "head", m
        )
        for m in range(1, nh)
    ]
    y0 = swapped(d0[1]) if whole else returned(d0[0])
    o1, *d1 = attention(whole, base1, codes, counts, qg1, kv1)
    if not whole:
        d0, d1 = [y0], [returned(d1[0])]
    y_slots = (nz if whole else 1, group, pair)
    slots = (nz if whole else 1, 2, group, pair)
    return pl.pallas_call(
        functools.partial(leave, nh, nblk, whole),
        out_shape=(
            like(query.shape, bf16), like(query.shape, bf16),
            like(key.shape, bf16), like(value.shape, bf16),
        ),
        in_specs=[in_vmem] * 9,
        out_specs=[in_vmem] * 4,
        scratch_shapes=[
            pltpu.VMEM(y_slots, bf16), pltpu.VMEM(slots, bf16), pltpu.VMEM(slots, bf16),
            pltpu.VMEM(slots, bf16), pltpu.VMEM((group, 2 * pair), bf16),
            dma((4, nh - 1)), dma((4, nh - 1)),
            dma((nz, 2)), dma((nz, 2)), dma((nz, 2)), dma((nz, 2)),
            dma((nz,)), dma((nz,)),
        ],
        compiler_params=pltpu.CompilerParams(
            collective_id=1, has_side_effects=True, vmem_limit_bytes=40 * 2**20
        ),
    )(o0, *came, o1, d0[0], y0, d1[0], d1[-1])


def solution(mesh):
    tokens = P(("blk", "head"), None)
    return jax.shard_map(
        body,
        mesh=mesh,
        in_specs=(tokens,) * 4 + (P("blk", None, None), P("blk", None)),
        out_specs=(tokens,) * 4,
        check_vma=False,
    )
```

```python
import functools
import math

import jax
import jax.numpy as jnp
from jax import lax
from jax.experimental import pallas as pl
from jax.experimental.pallas import tpu as pltpu
from jax.sharding import PartitionSpec as P

QUERY_HEADS = 64
KEY_VALUE_HEADS = 8
HEAD_SIZE = 128
BLOCK = 128
NEGATIVE_FILL = -1e30

NT = (((1,), (1,)), ((), ()))
NN = (((1,), (0,)), ((), ()))
TN = (((0,), (0,)), ((), ()))
MESH = pl.DeviceIdType.MESH
LINE = 2


def dot(a, b, dims):
    return lax.dot_general(a, b, dims, preferred_element_type=jnp.float32)


def query_block(nblocks, base_ref, turn):
    return lax.rem(base_ref[1] + base_ref[2] * turn, nblocks)


def attend(
    nstep, nblocks, heads, split, inputs, base_ref, codes_ref, counts_ref, *refs
):
    asked, (k_ref, v_ref, out_ref) = refs[:inputs], refs[inputs : inputs + 3]
    shares = 2 if split else 1
    dkv_refs = refs[inputs + 3 : inputs + 3 + shares]
    lst, cnt, qs, gs, scores, out_t, dq_t, dk, dv = refs[inputs + 3 + shares :]

    def place_of(base, s):
        at = lax.rem(base - s + nstep, nstep)
        if not split:
            return at
        far = lax.rem(at + base, LINE)
        return at // LINE + far * (nstep // LINE)

    scale = HEAD_SIZE ** (-0.5)
    c2 = scale * math.log2(math.e)
    turn = pl.program_id(0)
    qb = query_block(nblocks, base_ref, turn)
    width = heads * BLOCK
    room = nstep * nblocks
    both = 2 * BLOCK
    f32, bf16 = jnp.float32, jnp.bfloat16

    @pl.when(turn == 0)
    def _():
        dk[...] = jnp.zeros_like(dk)
        dv[...] = jnp.zeros_like(dv)
        base = base_ref[0]
        for b in range(nblocks):
            cnt[b] = 1
            lst[b * room] = place_of(base, 0) * nblocks + b

        def over_steps(s, _):
            place = place_of(base, s) * nblocks

            def over_codes(i, _):
                code = codes_ref[s, i]
                row = code // nblocks
                col = code - row * nblocks

                @pl.when(jnp.logical_or(s != 0, row != col))
                def _():
                    n = cnt[row]
                    lst[row * room + n] = place + col
                    cnt[row] = n + 1

                return 0

            return lax.fori_loop(0, counts_ref[s], over_codes, 0)

        lax.fori_loop(0, nstep, over_steps, 0)

    n = cnt[qb]
    first = qb * room
    chunks = (n + 1) // 2

    def rows_of(i):
        at = lst[first + jnp.where(i < n, i, 0)]
        return pl.ds(pl.multiple_of(at * BLOCK, BLOCK), BLOCK)

    def two(ref, c):
        return jnp.concatenate([ref[rows_of(2 * c), :], ref[rows_of(2 * c + 1), :]], axis=0)

    def turned(x):
        return jnp.transpose(x.astype(f32)).astype(bf16)

    def load(q_ref, g_ref, g_at):
        for h in range(heads):
            cols = slice(h * BLOCK, (h + 1) * BLOCK)
            qs[cols, :] = q_ref[:, cols]
            gs[cols, :] = g_ref[:, g_at + h * BLOCK : g_at + (h + 1) * BLOCK]

    if inputs == 2:
        load(asked[0], asked[1], 0)
    else:
        for m in range(inputs):
            pl.when(turn == m)(functools.partial(load, asked[m], asked[m], width))

    tiles = [slice(t * both, (t + 1) * both) for t in range(width // both)]

    def tile_top(s, cols, c, top):
        scores[c, :, cols] = s
        return jnp.maximum(top, jnp.max(s, axis=0, keepdims=True))

    def ending(s, c):
        last = jnp.where(2 * c + 1 < n, s[BLOCK:], NEGATIVE_FILL)
        return jnp.concatenate([s[:BLOCK], last], axis=0)

    key_at = lax.broadcasted_iota(jnp.int32, (both, both), 0)
    query_at = lax.broadcasted_iota(jnp.int32, (both, both), 1) % BLOCK
    seen = jnp.logical_or(key_at <= query_at, key_at >= BLOCK)
    kk = two(k_ref, 0)
    tops = []
    for cols in tiles:
        s = jnp.where(seen, dot(kk, qs[cols, :], NT), NEGATIVE_FILL)
        tops.append(tile_top(ending(s, 0), cols, 0, jnp.full((1, both), NEGATIVE_FILL, f32)))

    def score_pass(c, tops):
        kk = two(k_ref, c)
        return tuple(
            tile_top(ending(dot(kk, qs[cols, :], NT), c), cols, c, top)
            for cols, top in zip(tiles, tops)
        )

    tops = lax.fori_loop(1, chunks, score_pass, tuple(tops))
    out_t[...] = jnp.zeros_like(out_t)

    def weight_pass(c, totals):
        vt = turned(two(v_ref, c))
        new = []
        for cols, top, total in zip(tiles, tops, totals):
            w = jnp.exp2((scores[c, :, cols] - top) * c2)
            scores[c, :, cols] = w
            out_t[:, cols] += dot(vt, w.astype(bf16), NN)
            new.append(total + jnp.sum(w, axis=0, keepdims=True))
        return tuple(new)

    zero = tuple(jnp.zeros((1, both), f32) for _ in tiles)
    totals = lax.fori_loop(0, chunks, weight_pass, zero)
    invs = [1.0 / total for total in totals]

    row_dots = []
    for h in range(heads):
        cols = slice(h * BLOCK, (h + 1) * BLOCK)
        inv = invs[h // 2][:, (h % 2) * BLOCK : (h % 2 + 1) * BLOCK]
        attn = jnp.transpose(out_t[:, cols] * inv).astype(bf16)
        out_ref[:, cols] = attn
        prod = attn.astype(f32) * gs[cols, :].astype(f32)
        row_dots.append(jnp.sum(jnp.transpose(prod), axis=0, keepdims=True))
    row_dots = [
        jnp.concatenate(row_dots[2 * t : 2 * t + 2], axis=1) for t in range(len(tiles))
    ]
    dq_t[...] = jnp.zeros_like(dq_t)

    def grad_pass(c, _):
        kt = turned(two(k_ref, c))
        vv = two(v_ref, c)
        dv_now = jnp.zeros((both, HEAD_SIZE), f32)
        dk_now = jnp.zeros((both, HEAD_SIZE), f32)
        for cols, inv, row_dot in zip(tiles, invs, row_dots):
            p = scores[c, :, cols] * inv
            dv_now += dot(p.astype(bf16), gs[cols, :], NN)
            dp = dot(vv, gs[cols, :], NT)
            ds = (p * (dp - row_dot)).astype(bf16)
            dk_now += dot(ds, qs[cols, :], NN)
            dq_t[:, cols] += dot(kt, ds, NN)
        for i in range(2):
            rows = rows_of(2 * c + i)
            part = slice(i * BLOCK, (i + 1) * BLOCK)
            dv[rows, :] += dv_now[part]
            dk[rows, :] += dk_now[part]
        return 0

    lax.fori_loop(0, chunks, grad_pass, 0)
    for h in range(heads):
        cols = slice(h * BLOCK, (h + 1) * BLOCK)
        out_ref[:, width + h * BLOCK : width + (h + 1) * BLOCK] = jnp.transpose(
            dq_t[:, cols] * scale
        ).astype(bf16)

    @pl.when(turn == nblocks - 1)
    def _():
        for share, ref in enumerate(dkv_refs):
            rows = slice(share * ref.shape[0], (share + 1) * ref.shape[0])
            ref[:, :HEAD_SIZE] = (dk[rows, :] * scale).astype(bf16)
            ref[:, HEAD_SIZE:] = dv[rows, :].astype(bf16)


def attention(split, base, codes, counts, asked, kv):
    nstep = codes.shape[0]
    inputs = len(asked)
    width = HEAD_SIZE * (QUERY_HEADS // KEY_VALUE_HEADS)
    heads = width // HEAD_SIZE
    rows = asked[0].shape[0] * (1 if inputs == 2 else inputs)
    nblocks = rows // BLOCK
    keys = kv.shape[0]
    shares = 2 if split else 1
    f32, bf16 = jnp.float32, jnp.bfloat16
    flops = 6 * 2 * 30 * width * BLOCK * HEAD_SIZE
    whole_block = lambda i, *_: (0, 0)
    if inputs == 2:
        q_specs = [pl.BlockSpec((BLOCK, width), lambda i, *_: (i, 0))] * 2
    else:
        q_specs = [pl.BlockSpec((BLOCK, 2 * width), whole_block)] * inputs
    return pl.pallas_call(
        functools.partial(attend, nstep, nblocks, heads, split, inputs),
        out_shape=[jax.ShapeDtypeStruct((rows, 2 * width), bf16)]
        + [jax.ShapeDtypeStruct((keys // shares, 2 * HEAD_SIZE), bf16)] * shares,
        grid_spec=pltpu.PrefetchScalarGridSpec(
            num_scalar_prefetch=3,
            grid=(nblocks,),
            in_specs=q_specs
            + [
                pl.BlockSpec((keys, HEAD_SIZE), whole_block),
                pl.BlockSpec((keys, HEAD_SIZE), lambda i, *_: (0, 1)),
            ],
            out_specs=[
                pl.BlockSpec(
                    (BLOCK, 2 * width),
                    lambda i, base, *_: (query_block(nblocks, base, i), 0),
                ),
            ]
            + [pl.BlockSpec((keys // shares, 2 * HEAD_SIZE), whole_block)] * shares,
            scratch_shapes=[
                pltpu.SMEM((nblocks * nstep * nblocks,), jnp.int32),
                pltpu.SMEM((nblocks,), jnp.int32),
                pltpu.VMEM((width, HEAD_SIZE), bf16),
                pltpu.VMEM((width, HEAD_SIZE), bf16),
                pltpu.VMEM((nstep * nblocks // 2, 2 * BLOCK, width), f32),
                pltpu.VMEM((HEAD_SIZE, width), f32),
                pltpu.VMEM((HEAD_SIZE, width), f32),
                pltpu.VMEM((keys, HEAD_SIZE), f32),
                pltpu.VMEM((keys, HEAD_SIZE), f32),
            ],
        ),
        compiler_params=pltpu.CompilerParams(vmem_limit_bytes=48 * 2**20),
        cost_estimate=pl.CostEstimate(
            flops=16 * flops, bytes_accessed=2**23, transcendentals=30 * width * BLOCK
        ),
    )(base, codes, counts, *asked, kv, kv)


def greet(nh, nblk, whole, me, blk):
    barrier = pltpu.get_barrier_semaphore()
    for m in range(1, nh):
        pl.semaphore_signal(
            barrier, inc=1, device_id=(lax.rem(me + m, nh), blk), device_id_type=MESH
        )
    others = nblk if whole else 1
    for m in range(1, others):
        pl.semaphore_signal(
            barrier, inc=1, device_id=(me, lax.rem(blk + m, nblk)), device_id_type=MESH
        )
    pl.semaphore_wait(barrier, nh - 1 + others - 1)


def aligned(index, size):
    return pl.ds(pl.multiple_of(index * size, size), size)


def remote(src, dst, sems, device):
    return pltpu.make_async_remote_copy(
        src_ref=src, dst_ref=dst, send_sem=sems[0], recv_sem=sems[1],
        device_id=device, device_id_type=MESH,
    )


def enter(
    nh, nblk, whole, q, k, v, g, q0, g0, kv0, kv1, *refs
):
    cuts = refs[:nh]
    send, recv, up_s, up_r, down_s, down_r, y_s, y_r = refs[nh:]
    me, blk = lax.axis_index("head"), lax.axis_index("blk")
    greet(nh, nblk, whole, me, blk)
    rows = q.shape[0]
    qc = q0.shape[1]
    group = nh * rows
    nz = nblk // LINE
    hi, lo = blk // LINE, lax.rem(blk, LINE)
    keys = (kv0, kv1)

    def parts(n):
        if n < 4:
            j, which = n // 2, n % 2
            at = aligned((hi * nh if whole else 0) + me, rows)
            dst = keys[j].at[at, pl.ds(which * HEAD_SIZE, HEAD_SIZE)]
            return (k, v)[which], HEAD_SIZE, j, dst
        return (q, g)[n - 4], qc, 0, (q0, g0)[n - 4].at[aligned(me, rows), :]

    def to_peer(n, m):
        src, cols, j, dst = parts(n)
        peer = lax.rem(me + m, nh)
        return remote(
            src.at[:, aligned(peer * 2 + j, cols)], dst,
            (send.at[n, m - 1], recv.at[n, m - 1]), (peer, blk),
        )

    def own(n):
        src, cols, j, dst = parts(n)
        dst[...] = src[:, aligned(me * 2 + j, cols)]

    order = (2, 3, 1) if nh == 4 else tuple(range(1, nh))

    def start(n):
        for m in order:
            to_peer(n, m).start()

    def arrived(n):
        for m in order:
            to_peer(n, m).wait_recv()

    def block(j, z):
        return keys[j].at[aligned(z, group), :]

    def up(j, d):
        return remote(
            block(j, hi - d), block(j, hi - d), (up_s.at[j, d], up_r.at[j, d]),
            (me, blk + LINE),
        )

    def down(j, d):
        return remote(
            block(j, hi + d), block(j, hi + d), (down_s.at[j, d], down_r.at[j, d]),
            (me, blk - LINE),
        )

    def across(z, slot):
        return remote(
            block(0, z), block(0, nz + z), (y_s.at[slot], y_r.at[slot]),
            (me, blk + 1 - 2 * lo),
        )

    def pass_on(j, d):
        if d > 0:
            pl.when(hi - d >= 0)(lambda: up(j, d - 1).wait_recv())
        if d < nz - 1:
            pl.when(jnp.logical_and(hi - d >= 0, hi < nz - 1))(lambda: up(j, d).start())
        if d > 0:
            pl.when(hi + d < nz)(lambda: down(j, d - 1).wait_recv())
        if d < nz - 1:
            pl.when(jnp.logical_and(hi + d < nz, hi > 0))(lambda: down(j, d).start())
        if j > 0:
            return
        if d == 0:
            across(hi, 0).start()
        else:
            pl.when(hi - d >= 0)(lambda: across(hi - d, d).start())
            pl.when(hi + d < nz)(lambda: across(hi + d, nz - 1 + d).start())

    for n in range(4):
        start(n)
    for n in range(4):
        own(n)
    for j in range(2):
        arrived(2 * j)
        arrived(2 * j + 1)
        if whole:
            pass_on(j, 0)
    start(4)
    start(5)

    own(4)
    own(5)
    for m in range(nh):
        at = aligned(lax.rem(me + m, nh) * 2 + 1, qc)
        cuts[m][:, :qc] = q[:, at]
        cuts[m][:, qc:] = g[:, at]
    if whole:
        for d in range(1, nz):
            pass_on(0, d)
            pass_on(1, d)
        across(hi, 0).wait()
        for d in range(1, nz):
            pl.when(hi - d >= 0)(lambda d=d: across(hi - d, d).wait())
            pl.when(hi + d < nz)(lambda d=d: across(hi + d, nz - 1 + d).wait())
        for j in range(2):
            for d in range(nz - 1):
                pl.when(jnp.logical_and(hi - d >= 0, hi < nz - 1))(
                    lambda j=j, d=d: up(j, d).wait_send()
                )
                pl.when(jnp.logical_and(hi + d < nz, hi > 0))(
                    lambda j=j, d=d: down(j, d).wait_send()
                )
    arrived(4)
    arrived(5)
    for n in range(6):
        for m in order:
            to_peer(n, m).wait_send()


def leave(
    nh, nblk, whole, o0, r1, r2, r3, o1, d0, y0, d1, far, attn, dq, dk, dv,
    y_in, up_in, down_in, sums, home, send, recv,
    up_s, up_r, down_s, down_r, y_s, y_r,
):
    me, blk = lax.axis_index("head"), lax.axis_index("blk")
    greet(nh, nblk, whole, me, blk)
    grads = (d0, d1)
    rows = attn.shape[0]
    group = nh * rows
    half = o1.shape[1] // 2
    kw = dk.shape[1] // nh
    f32, bf16 = jnp.float32, jnp.bfloat16
    nz = nblk // LINE
    hi, lo = blk // LINE, lax.rem(blk, LINE)

    def part(n, row):
        if n < 2:
            return (
                o1.at[aligned(row, rows), pl.ds(n * half, half)],
                (attn, dq)[n].at[:, aligned(me * 2 + 1, half)],
            )
        return (
            home.at[aligned(row, rows), pl.ds((n - 2) * kw, kw)],
            (dk, dv)[n - 2].at[:, aligned(me, kw)],
        )

    def to_peer(n, m):
        peer = lax.rem(me + m, nh)
        src, dst = part(n, peer)
        return remote(src, dst, (send.at[n, m - 1], recv.at[n, m - 1]), (peer, blk))

    def own(n):
        src, dst = part(n, me)
        dst[...] = src[...]

    def brought(m, which):
        cols = pl.ds(which * half, half)
        src = o0.at[aligned(me, rows), cols] if m == 0 else (r1, r2, r3)[m - 1].at[:, cols]
        to = aligned(lax.rem(me - m + nh, nh) * 2, half)
        (attn, dq)[which][:, to] = src[...]

    order = (2, 3, 1) if nh == 4 else tuple(range(1, nh))

    def across(z):
        return remote(
            far.at[pl.ds(z * group, group), :], y_in.at[z], (y_s.at[z], y_r.at[z]),
            (me, blk + 1 - 2 * lo),
        )

    def start_outs():
        for n in range(2):
            for m in order:
                to_peer(n, m).start()

    def bring_outs():
        for n in range(2):
            own(n)
        for m in range(nh):
            for which in range(2):
                brought(m, which)

    def up(z, j):
        return remote(
            sums.at[z, j], up_in.at[z, j], (up_s.at[z, j], up_r.at[z, j]), (me, blk + LINE)
        )

    def down(z, j):
        return remote(
            sums.at[z, j], down_in.at[z, j], (down_s.at[z, j], down_r.at[z, j]),
            (me, blk - LINE),
        )

    def mine(z, j):
        at = pl.ds(z * group, group)
        came = y0[at, :] if j == 0 else y_in[z]
        return grads[j][at, :].astype(f32) + came.astype(f32)

    def finish(j, value):
        for which in range(2):
            at = which * 2 + j
            home[:, at * HEAD_SIZE : (at + 1) * HEAD_SIZE] = value[
                :, which * HEAD_SIZE : (which + 1) * HEAD_SIZE
            ].astype(bf16)

    def hop(z, j, copy, first, arrivals):
        @pl.when(hi == first)
        def _():
            sums[z, j] = mine(z, j).astype(bf16)

        @pl.when(hi != first)
        def _():
            copy(z, j).wait_recv()
            sums[z, j] = (mine(z, j) + arrivals[z, j].astype(f32)).astype(bf16)

        copy(z, j).start()

    if whole:
        def chains(order):
            for z in order:
                across(z).start()
            start_outs()
            for j in range(2):
                for z in order:
                    if j == 1:
                        across(z).wait_recv()
                    pl.when(hi < z)(functools.partial(hop, z, j, up, 0, up_in))
                    pl.when(hi > z)(functools.partial(hop, z, j, down, nz - 1, down_in))

        def ends_first(places):
            return [places[i // 2] if i % 2 == 0 else places[-1 - i // 2] for i in range(nz)]

        upward = ends_first(list(range(nz - 1, -1, -1)))
        pl.when(hi < nz // 2)(functools.partial(chains, upward))
        pl.when(hi >= nz // 2)(functools.partial(chains, ends_first(list(range(nz)))))
        for j in range(2):
            for z in range(nz):
                @pl.when(hi == z)
                def _(z=z, j=j):
                    value = mine(z, j)
                    if z > 0:
                        up(z, j).wait_recv()
                        value += up_in[z, j].astype(f32)
                    if z < nz - 1:
                        down(z, j).wait_recv()
                        value += down_in[z, j].astype(f32)
                    finish(j, value)

    else:
        start_outs()
        for j in range(2):
            finish(j, grads[j][...].astype(f32))
    for n in (2, 3):
        for m in order:
            to_peer(n, m).start()
        own(n)
    bring_outs()
    if whole:
        for z in range(nz):
            across(z).wait_send()
            for j in range(2):
                pl.when(hi < z)(lambda z=z, j=j: up(z, j).wait_send())
                pl.when(hi > z)(lambda z=z, j=j: down(z, j).wait_send())
    for n in range(4):
        for m in order:
            to_peer(n, m).wait()


def permuted(block, axis, distance):
    size = lax.axis_size(axis)
    return lax.ppermute(block, axis, [(i, (i + distance) % size) for i in range(size)])


def swapped(block):
    return lax.ppermute(block, "blk", [(i, i ^ 1) for i in range(lax.axis_size("blk"))])


def body(query, key, value, output_gradient, pair_codes, pair_counts):
    rows = query.shape[0]
    nh = lax.axis_size("head")
    nblk = lax.axis_size("blk")
    codes, counts = pair_codes[0], pair_counts[0]
    nstep = codes.shape[0]
    whole = nblk == nstep
    nz = nblk // LINE
    group = nh * rows
    bf16 = jnp.bfloat16
    dma = pltpu.SemaphoreType.DMA
    in_vmem = pl.BlockSpec(memory_space=pltpu.VMEM)
    width = query.shape[1] // KEY_VALUE_HEADS
    pair = 2 * HEAD_SIZE
    like = jax.ShapeDtypeStruct
    q0, g0, kv0, kv1, *cuts = pl.pallas_call(
        functools.partial(enter, nh, nblk, whole),
        out_shape=(
            like((group, width), bf16),
            like((group, width), bf16),
            like((group * (nblk if whole else 1), pair), bf16),
            like((group * (nz if whole else 1), pair), bf16),
        )
        + (like((rows, 2 * width), bf16),) * nh,
        in_specs=[in_vmem] * 4,
        out_specs=[in_vmem] * (4 + nh),
        scratch_shapes=[
            dma((6, nh - 1)), dma((6, nh - 1)),
            dma((2, nz)), dma((2, nz)), dma((2, nz)), dma((2, nz)),
            dma((2 * nz,)), dma((2 * nz,)),
        ],
        compiler_params=pltpu.CompilerParams(
            collective_id=0, has_side_effects=True, vmem_limit_bytes=40 * 2**20
        ),
    )(query, key, value, output_gradient)
    me = lax.axis_index("head")
    if whole:
        kv1 = jnp.concatenate([kv1, swapped(kv1)], axis=0)
    else:
        kv0, kv1 = (
            jnp.concatenate(
                [kv] + [permuted(kv, "blk", nstep - i) for i in range(1, nstep)], axis=0
            )
            for kv in (kv0, kv1)
        )
    qg1 = [cuts[0]] + [permuted(cuts[m], "head", m) for m in range(1, nh)]
    start = lax.axis_index("blk") if whole else jnp.int32(0)
    base0 = jnp.stack([start, jnp.int32(0), jnp.int32(1)]).astype(jnp.int32)
    base1 = jnp.stack([start, me, jnp.int32(nh - 1)]).astype(jnp.int32)

    def returned(grad):
        if whole:
            return grad
        parts = grad.reshape(nstep, group, -1)
        total = parts[0].astype(jnp.float32)
        for i in range(1, nstep):
            total += permuted(parts[i], "blk", i - nstep).astype(jnp.float32)
        return total.astype(bf16)

    o0, *d0 = attention(whole, base0, codes, counts, [q0, g0], kv0)
    came = [
        permuted(
            lax.dynamic_slice_in_dim(o0, lax.rem(me + m, nh) * rows, rows, 0), "head", m
        )
        for m in range(1, nh)
    ]
    y0 = swapped(d0[1]) if whole else returned(d0[0])
    o1, *d1 = attention(whole, base1, codes, counts, qg1, kv1)
    if not whole:
        d0, d1 = [y0], [returned(d1[0])]
    y_slots = (nz if whole else 1, group, pair)
    slots = (nz if whole else 1, 2, group, pair)
    return pl.pallas_call(
        functools.partial(leave, nh, nblk, whole),
        out_shape=(
            like(query.shape, bf16), like(query.shape, bf16),
            like(key.shape, bf16), like(value.shape, bf16),
        ),
        in_specs=[in_vmem] * 9,
        out_specs=[in_vmem] * 4,
        scratch_shapes=[
            pltpu.VMEM(y_slots, bf16), pltpu.VMEM(slots, bf16), pltpu.VMEM(slots, bf16),
            pltpu.VMEM(slots, bf16), pltpu.VMEM((group, 2 * pair), bf16),
            dma((4, nh - 1)), dma((4, nh - 1)),
            dma((nz, 2)), dma((nz, 2)), dma((nz, 2)), dma((nz, 2)),
            dma((nz,)), dma((nz,)),
        ],
        compiler_params=pltpu.CompilerParams(
            collective_id=1, has_side_effects=True, vmem_limit_bytes=40 * 2**20
        ),
    )(o0, *came, o1, d0[0], y0, d1[0], d1[-1])


def solution(mesh):
    tokens = P(("blk", "head"), None)
    return jax.shard_map(
        body,
        mesh=mesh,
        in_specs=(tokens,) * 4 + (P("blk", None, None), P("blk", None)),
        out_specs=(tokens,) * 4,
        check_vma=False,
    )
```
